32 devices in a mesh: groups: 2 (over y), batch: 4 (over z), tensor: 4 (over x, core).
Axes of the slice: x: 2, y: 2, z: 4, core: 2. Of those that a mesh axis runs over, the one named last changes fastest.
Arguments:
- session_head_state: bfloat16 [128, 64, 64, 128], P(('groups', 'batch'), 'tensor'), parts along dimension 0, may hold values from -4 to 4
- convolved_activation: bfloat16 [2, 128, 4096], P(None, ('groups', 'batch'), 'tensor'), parts along dimension 1, may hold values from -6 to 6
- gate_activations: bfloat16 [2, 128, 4096], P(None, ('groups', 'batch'), 'tensor'), parts along dimension 1, may hold values from -6 to 6
- state_input_projection: bfloat16 [2, 128, 4, 128], P(None, ('groups', 'batch')), parts along dimension 1, may hold values from -6 to 6
- state_output_projection: bfloat16 [2, 128, 4, 128], P(None, ('groups', 'batch')), parts along dimension 1, may hold values from -6 to 6
- raw_step_sizes: float32 [2, 128, 64], P(None, ('groups', 'batch'), 'tensor'), parts along dimension 1, may hold values from -3 to 3
- step_size_bias: float32 [64], P('tensor'), may hold values from -4 to -1
- log_decay_rate: float32 [64], P('tensor'), may hold values from 0 to 3
- skip_coefficient: float32 [64], P('tensor'), may hold values from 0.5 to 2
- group_norm_gain: bfloat16 [4096], P('tensor'), may hold values from 0.5 to 1.5
- adapter_down_weight: bfloat16 [16, 64, 4096], P(('groups', 'batch'), None, 'tensor'), parts along dimension 0, may hold values from -0.09375 to 0.09375
- adapter_up_weight: bfloat16 [16, 64, 4096], P(('groups', 'batch'), None, 'tensor'), parts along dimension 0, may hold values from -0.75 to 0.75
- adapter_per_session: int32 [128], P(('groups', 'batch')), parts along dimension 0, may hold values from 0 to 7, as said below
- adapter_storage_slot: int32 [16], P('groups'), parts along dimension 0, may hold values from 0 to 7, as said below
Outputs:
- updated_state: bfloat16 [128, 64, 64, 128], P(('groups', 'batch'), 'tensor'), parts along dimension 0
- normed: bfloat16 [2, 128, 4096], P(None, ('groups', 'batch'), 'tensor'), parts along dimension 1
- adapter_output_term: float32 [2, 128, 4096], P(None, ('groups', 'batch'), 'tensor'), parts along dimension 1
The draws below stay inside these ranges and needn't reach their ends.
There are 2 independent parts, one for each index of `groups`. The reference program is written for one: setup_inputs(seed, part) draws one part's arguments, and reference() takes and returns one part's arrays. A program takes and returns all parts, laid end to end along the dimension named above; an argument that names none is the same for every part. Nothing has to cross between parts.
Inputs may be any that keep to these rules, and one draw needn't show every extreme that they name: A permutation: adapter a is stored in slot adapter_storage_slot[a] of adapter_down_weight and adapter_up_weight, held by batch index adapter_storage_slot[a] // 2. `adapter_per_session`: the sessions of one batch index use adapters of one owner at most 4 times; in every draw one owner is used exactly 4 times by the sessions of every batch index.
All inputs are finite; a program needn't handle non-finite values.
Results may differ from the reference program's by a relative error of at most 0.0053.
Values may be sent and summed in bfloat16 or wider, within the bound.
No kernel may reach another device: no remote copies, remote signals or barrier semaphores. Data moves between devices by JAX's collectives and lax.ppermute only.
A program may use at most 64 MiB of HBM per device.

```python
import jax
import jax.numpy as jnp
from jax import lax

MODEL_WIDTH = 4096
HEAD_COUNT = 64
HEAD_CHANNELS = 64
STATE = 128
GROUPS = 4
ADAPTER_RANK = 64
DECODE_STEPS = 2
ADP_DEV = 2
S_DEV = 16
SESSION_TOTAL = 64
ADAPTER_TOTAL = 8
CAP = 4
N_BATCH = 4


def routing_tables(key):
    perm_key, hot_key, rest_key, within_key = jax.random.split(key, 4)
    slot_of = jax.random.permutation(perm_key, ADAPTER_TOTAL).astype(jnp.int32)
    hottest = jax.random.randint(hot_key, (), 0, N_BATCH).astype(jnp.int32)

    def block_owners(block_key):
        key_one, key_two = jax.random.split(block_key)
        places = jax.random.permutation(key_one, (N_BATCH - 1) * CAP).astype(jnp.int32)[:S_DEV - CAP]
        others = (hottest + 1 + places // CAP) % N_BATCH
        owners = jnp.concatenate([jnp.full((CAP,), hottest, dtype=jnp.int32), others.astype(jnp.int32)])
        return jax.random.permutation(key_two, owners)
    owners = jax.vmap(block_owners)(jax.random.split(rest_key, N_BATCH)).reshape(-1)
    within = jax.random.randint(within_key, (SESSION_TOTAL,), 0, ADP_DEV).astype(jnp.int32)
    slots = owners * ADP_DEV + within
    adapter_at = jnp.zeros((ADAPTER_TOTAL,), jnp.int32).at[slot_of].set(jnp.arange(ADAPTER_TOTAL, dtype=jnp.int32))
    return (slot_of, adapter_at[slots])


def draw_adapter_per_session(key, part):
    return routing_tables(key)[1]


def draw_adapter_storage_slot(key, part):
    return routing_tables(key)[0]


def shard_levels(rng, extent, pieces, smallest, top_value):
    def one(dim, shards_of):
        draws = jax.random.uniform(jax.random.fold_in(jax.random.fold_in(rng, 6), dim), (shards_of,), jnp.float32, smallest / len(pieces), top_value / len(pieces))
        return jnp.repeat(jnp.exp(draws), extent[dim] // shards_of).reshape((-1,) + (1,) * (len(extent) - dim - 1))

    factor_of = one(*pieces[0])
    for cut in pieces[1:]:
        factor_of = factor_of * one(*cut)
    return factor_of


def bell_draw(stream_key, extent, width, reach, shards=(), kind=jnp.bfloat16):
    values = width * jax.random.normal(stream_key, extent, jnp.float32)
    if shards:
        values = values * shard_levels(stream_key, extent, shards, -0.22, 0.18)
    return jnp.clip(values, -reach, reach).astype(kind)


def setup_inputs(seed: int = 0, part: int = 0) -> dict:
    seeds = jax.random.split(jax.random.key(seed), 15)
    part_splits = jax.random.split(jax.random.fold_in(seeds[14], part), 15)
    return {
        "session_head_state": bell_draw(part_splits[0], (SESSION_TOTAL, HEAD_COUNT, HEAD_CHANNELS, STATE), 0.5, 4.0, ((0, 4), (1, 4))),
        "convolved_activation": bell_draw(part_splits[1], (DECODE_STEPS, SESSION_TOTAL, HEAD_COUNT * HEAD_CHANNELS), 1.0, 6.0, ((1, 4), (2, 4))),
        "gate_activations": bell_draw(part_splits[2], (DECODE_STEPS, SESSION_TOTAL, HEAD_COUNT * HEAD_CHANNELS), 1.0, 6.0, ((1, 4), (2, 4))),
        "state_input_projection": bell_draw(part_splits[3], (DECODE_STEPS, SESSION_TOTAL, GROUPS, STATE), 1.0, 6.0, ((1, 4),)),
        "state_output_projection": bell_draw(part_splits[4], (DECODE_STEPS, SESSION_TOTAL, GROUPS, STATE), 1.0, 6.0, ((1, 4),)),
        "raw_step_sizes": bell_draw(part_splits[5], (DECODE_STEPS, SESSION_TOTAL, HEAD_COUNT), 0.5, 3.0, ((1, 4), (2, 4)), jnp.float32),
        "step_size_bias": jnp.clip(-4.0 + 3.0 * jax.random.uniform(seeds[6], (HEAD_COUNT,), jnp.float32) ** shard_levels(seeds[6], (HEAD_COUNT,), ((0, 4),), -0.2, 0.2), -4.0, -1.0),
        "log_decay_rate": jnp.clip(3.0 * jax.random.uniform(seeds[7], (HEAD_COUNT,), jnp.float32) ** shard_levels(seeds[7], (HEAD_COUNT,), ((0, 4),), -0.2, 0.2), 0.0, 3.0),
        "skip_coefficient": jnp.clip(0.5 + 1.5 * jax.random.uniform(seeds[8], (HEAD_COUNT,), jnp.float32) ** shard_levels(seeds[8], (HEAD_COUNT,), ((0, 4),), -0.2, 0.2), 0.5, 2.0),
        "group_norm_gain": jnp.clip(1.0 + 0.1 * jax.random.normal(seeds[9], (HEAD_COUNT * HEAD_CHANNELS,), jnp.float32), 0.5, 1.5).astype(jnp.bfloat16),
        "adapter_down_weight": bell_draw(part_splits[10], (ADAPTER_TOTAL, ADAPTER_RANK, HEAD_COUNT * HEAD_CHANNELS), (HEAD_COUNT * HEAD_CHANNELS) ** -0.5, 0.09375, ((0, 4), (2, 4))),
        "adapter_up_weight": bell_draw(part_splits[11], (ADAPTER_TOTAL, ADAPTER_RANK, MODEL_WIDTH), ADAPTER_RANK ** -0.5, 0.75, ((0, 4), (2, 4))),
        "adapter_per_session": draw_adapter_per_session(jax.random.fold_in(jax.random.fold_in(seeds[14], part), 71), part),
        "adapter_storage_slot": draw_adapter_storage_slot(jax.random.fold_in(jax.random.fold_in(seeds[14], part), 71), part),
    }


adapter_scale = 2.0
norm_eps = 1e-05

def reference(session_head_state, convolved_activation, gate_activations, state_input_projection, state_output_projection, raw_step_sizes, step_size_bias, log_decay_rate, skip_coefficient, group_norm_gain, adapter_down_weight, adapter_up_weight, adapter_per_session, adapter_storage_slot):
    group_heads = HEAD_COUNT // GROUPS
    inner_activation = HEAD_COUNT * HEAD_CHANNELS
    gain = group_norm_gain.astype(jnp.float32)
    highest_precision = lax.Precision.HIGHEST

    def advance(operands):
        block_state, block_x, block_z, block_b, block_c, block_dt = operands
        carried = block_state.astype(jnp.float32)
        normed_list = []
        rounded = block_state
        for step_index in range(DECODE_STEPS):
            step_size = jax.nn.softplus(block_dt[step_index] + step_size_bias)
            decays = jnp.exp(-jnp.exp(log_decay_rate) * step_size)
            b_heads = jnp.repeat(block_b[step_index].astype(jnp.float32), group_heads, axis=1)
            c_heads = jnp.repeat(block_c[step_index].astype(jnp.float32), group_heads, axis=1)
            inputs = block_x[step_index].astype(jnp.float32).reshape(S_DEV, HEAD_COUNT, HEAD_CHANNELS)
            carried = decays[:, :, None, None] * carried + (step_size[:, :, None] * inputs)[:, :, :, None] * b_heads[:, :, None, :]
            outputs = jnp.einsum('shpn,shn->shp', carried, c_heads, precision=highest_precision) + skip_coefficient[None, :, None] * inputs
            gated_out = outputs.reshape(S_DEV, inner_activation) * jax.nn.silu(block_z[step_index].astype(jnp.float32))
            scaled = gated_out * lax.rsqrt(lax.optimization_barrier(jnp.mean(gated_out * gated_out, axis=1, keepdims=True)) + norm_eps)
            normed_list.append((scaled * gain).astype(jnp.bfloat16))
            rounded = lax.optimization_barrier(carried.astype(jnp.bfloat16))
            carried = rounded.astype(jnp.float32)
        return (rounded, jnp.stack(normed_list))

    def by_device(values):
        return values.reshape((DECODE_STEPS, N_BATCH, S_DEV) + values.shape[2:]).swapaxes(0, 1)
    updated_state, normed_all = lax.map(advance, (session_head_state.reshape((N_BATCH, S_DEV) + session_head_state.shape[1:]), by_device(convolved_activation), by_device(gate_activations), by_device(state_input_projection), by_device(state_output_projection), by_device(raw_step_sizes)))
    updated_state = updated_state.reshape(session_head_state.shape)
    normalized_rows = normed_all.swapaxes(0, 1).reshape(DECODE_STEPS * SESSION_TOTAL, inner_activation)
    slots = jnp.tile(adapter_storage_slot[adapter_per_session], DECODE_STEPS)

    def down_step(running, selected_slot):
        chosen = (slots == selected_slot).astype(jnp.float32)[:, None]
        update_term = jnp.dot(normalized_rows, adapter_down_weight[selected_slot].T, preferred_element_type=jnp.float32)
        return (running + chosen * update_term, None)
    rank_projected_rows, unused = lax.scan(down_step, jnp.zeros((DECODE_STEPS * SESSION_TOTAL, ADAPTER_RANK), jnp.float32), jnp.arange(ADAPTER_TOTAL, dtype=jnp.int32))
    rank_projected_rows = rank_projected_rows.astype(jnp.bfloat16)

    def up_step(running, selected_slot):
        chosen = (slots == selected_slot).astype(jnp.float32)[:, None]
        update_term = jnp.dot(rank_projected_rows, adapter_up_weight[selected_slot], preferred_element_type=jnp.float32)
        return (running + chosen * update_term, None)
    broadcast_rows, unused = lax.scan(up_step, jnp.zeros((DECODE_STEPS * SESSION_TOTAL, MODEL_WIDTH), jnp.float32), jnp.arange(ADAPTER_TOTAL, dtype=jnp.int32))
    adapter_output_term = (adapter_scale * broadcast_rows).reshape(DECODE_STEPS, SESSION_TOTAL, MODEL_WIDTH)
    return (updated_state, normalized_rows.reshape(DECODE_STEPS, SESSION_TOTAL, inner_activation), adapter_output_term)
```

```python
import functools

import jax
import jax.numpy as jnp
from jax import lax
from jax.experimental import pallas as pl
from jax.experimental.pallas import tpu as pltpu
from jax.sharding import PartitionSpec as P

HEAD_COUNT = 64
HEAD_CHANNELS = 64
GROUPS = 4
DECODE_STEPS = 2
RANK = 64
LANES = 128

adapter_scale = 2.0
norm_eps = 1e-05

F32 = jnp.float32
BF16 = jnp.bfloat16
HIGHEST = lax.Precision.HIGHEST
NT = (((1,), (1,)), ((), ()))


def iota(shape, axis):
    return lax.broadcasted_iota(jnp.int32, shape, axis)


def front_kernel(dims, *refs):
    sessions, heads, batch_count, capacity, adapters_held, chunks, split = dims
    (ids, adapter, slot_of, state, x, z, b, c, raw, bias, rate, skip, gain) = refs[:13]
    n_msg = batch_count if split else 1
    msgs = refs[13 : 13 + n_msg]
    gated_ref, square_ref, drive_ref, b_ref, keep_ref, place_ref = refs[13 + n_msg : 19 + n_msg]
    held, sems, counts = refs[19 + n_msg :]
    channels = heads * HEAD_CHANNELS
    rows = DECODE_STEPS * sessions
    part = heads // chunks
    width = part * HEAD_CHANNELS

    copies = []
    for i in range(chunks):
        window = pl.ds(i * part, part)
        copy = pltpu.make_async_copy(state.at[:, window], held.at[:, window], sems.at[i])
        copy.start()
        copies.append(copy)

    me = ids[0]
    group = ids[1]
    for i in range(batch_count):
        counts[i] = 0
    per_owner = DECODE_STEPS * capacity
    targets = batch_count * per_owner
    to = iota((targets, rows), 0)
    source = iota((targets, rows), 1)
    lane_to = iota((targets, LANES), 0)
    place = jnp.zeros((targets, rows), F32)
    pick = jnp.zeros((targets, LANES), F32)
    for s in range(sessions):
        slot = slot_of[adapter[s]]
        owner = slot // adapters_held
        which = (slot - owner * adapters_held).astype(F32)
        earlier = counts[owner]
        counts[owner] = earlier + 1
        relative = (owner ^ me) if split else owner
        first = relative * per_owner + earlier * DECODE_STEPS
        hit = (to - first == source // sessions) & (source % sessions == s)
        place = jnp.where(hit, 1.0, place)
        mine = (lane_to >= first) & (lane_to < first + DECODE_STEPS)
        pick = jnp.where(mine, which, pick)
    place_ref[...] = place
    place_bf = place.astype(BF16)

    def pick_group(ref):
        values = ref[...].astype(F32).reshape(rows, GROUPS, LANES)
        return jnp.sum(jnp.where(iota(values.shape, 1) == group, values, 0.0), axis=1)

    b_rows = pick_group(b)
    c_rows = pick_group(c)
    b_ref[...] = b_rows
    b1, b2 = b_rows[:sessions], b_rows[sessions:]
    c1, c2 = c_rows[:sessions], c_rows[sessions:]
    bc11 = jnp.sum(b1 * c1, axis=1, keepdims=True)
    bc12 = jnp.sum(b1 * c2, axis=1, keepdims=True)
    bc22 = jnp.sum(b2 * c2, axis=1, keepdims=True)

    def softplus(v):
        return jnp.maximum(v, 0.0) + jnp.log1p(jnp.exp(-jnp.abs(v)))

    step1 = softplus(raw[0] + bias[...])
    step2 = softplus(raw[1] + bias[...])
    speed = -jnp.exp(rate[...])
    decay1 = jnp.exp(speed * step1)
    decay2 = jnp.exp(speed * step2)
    keep = decay1 * decay2
    keep_ref[...] = keep
    factors = jnp.concatenate(
        [
            decay1,
            step1 * bc11 + skip[...],
            keep,
            decay2 * step1 * bc12,
            step2 * bc22 + skip[...],
            decay2 * step1,
            step2,
        ],
        axis=0,
    )
    spread = (iota((heads, channels), 1) // HEAD_CHANNELS == iota((heads, channels), 0)).astype(F32)
    wide = jnp.dot(factors, spread, precision=HIGHEST, preferred_element_type=F32)
    wide = [wide[i * sessions : (i + 1) * sessions] for i in range(7)]
    x1 = x[0].astype(F32)
    x2 = x[1].astype(F32)
    drive_ref[...] = jnp.concatenate([wide[5] * x1, wide[6] * x2], axis=0)
    base1 = x1 * wide[1]
    base2 = x1 * wide[3] + x2 * wide[4]
    gates = jnp.concatenate([z[0].astype(F32), z[1].astype(F32)], axis=0)
    gates = gates / (1.0 + jnp.exp(-gates))
    base = jnp.concatenate([base1, base2], axis=0)
    scale = jnp.concatenate([wide[0], wide[2]], axis=0)
    row_session = iota((rows, LANES), 0) % sessions
    c_blocks = jnp.concatenate(
        [jnp.where(row_session == s, c_rows, 0.0).astype(BF16) for s in range(sessions)], axis=1
    )
    squares = jnp.zeros((rows, LANES), F32)
    for i in range(chunks):
        copies[i].wait()
        lanes = slice(i * width, (i + 1) * width)
        block = jnp.concatenate(
            [
                held[s, i * part : (i + 1) * part].reshape(width, LANES)
                for s in range(sessions)
            ],
            axis=1,
        )
        reads = lax.dot_general(c_blocks, block, NT, preferred_element_type=F32)
        gated = (scale[:, lanes] * reads + base[:, lanes]) * gates[:, lanes]
        gated_ref[:, lanes] = gated
        for j in range(width // LANES):
            piece = gated[:, j * LANES : (j + 1) * LANES]
            squares = squares + piece * piece
        weighted = (gated * gain[:, lanes].astype(F32)).astype(BF16)
        packed = jnp.dot(place_bf, weighted, preferred_element_type=F32)
        for k in range(n_msg):
            n = targets // n_msg
            msgs[k][:, lanes] = packed[k * n : (k + 1) * n].astype(BF16)
    for k in range(n_msg):
        n = targets // n_msg
        msgs[k][:, channels:] = pick[k * n : (k + 1) * n].astype(BF16)
    square_ref[...] = squares[:, :RANK] + squares[:, RANK:]


def state_kernel(sessions, heads, pair, drive, b, keep, state, out, drive_t):
    i = pl.program_id(0)
    channels = heads * HEAD_CHANNELS
    rows = DECODE_STEPS * sessions

    @pl.when(i == 0)
    def _():
        turned = drive[...].T
        high = turned.astype(BF16)
        low = (turned - high.astype(F32)).astype(BF16)
        drive_t[...] = jnp.concatenate([high, low], axis=1)

    row_session = iota((rows, LANES), 0) % sessions
    b_rows = b[...]
    right = jnp.concatenate(
        [jnp.where(row_session == i * pair + q, b_rows, 0.0) for q in range(pair)], axis=1
    )
    right = jnp.concatenate([right, right], axis=0).astype(BF16)
    for h in range(heads):
        piece = slice(h * HEAD_CHANNELS, (h + 1) * HEAD_CHANNELS)
        added = jnp.dot(drive_t[piece], right, preferred_element_type=F32)
        for q in range(pair):
            kept = state[q, h].astype(F32) * keep[i * pair + q, h]
            out[q, h] = (kept + added[:, q * LANES : (q + 1) * LANES]).astype(BF16)


def down_kernel(n_msg, *refs):
    msgs = refs[:n_msg]
    down, squares, out, pick_ref = refs[n_msg:]
    held, rank, channels = down.shape
    rows = jnp.concatenate([m[...].astype(F32) for m in msgs], axis=0)
    pick = rows[:, channels:]
    weights = down[...].reshape(held * rank, channels)
    ranks = lax.dot_general(
        rows[:, :channels].astype(BF16), weights, NT, preferred_element_type=F32
    )
    chosen = jnp.zeros((rows.shape[0], rank), F32)
    for j in range(held):
        chosen = jnp.where(pick[:, :rank] == j, ranks[:, j * rank : (j + 1) * rank], chosen)
    pick_ref[...] = pick
    n_squares = squares.shape[0]
    if n_squares < chosen.shape[0]:
        filled = jnp.concatenate(
            [squares[...], jnp.zeros((chosen.shape[0] - n_squares, rank), F32)], axis=0
        )
    else:
        filled = squares[...]
    out[...] = jnp.concatenate([chosen, filled], axis=1)


def up_kernel(n_sum, n_msg, sessions, *refs):
    parts = refs[:n_sum]
    pick, up = refs[n_sum : n_sum + 2]
    outs = refs[n_sum + 2 : n_sum + 2 + n_msg]
    inverse = refs[n_sum + 2 + n_msg]
    held, rank, channels = up.shape
    total = parts[0][...]
    for p in parts[1:]:
        total = total + p[...]
    ranks = total[:, :rank]
    left = jnp.concatenate(
        [jnp.where(pick[:, :rank] == j, ranks, 0.0) for j in range(held)], axis=1
    ).astype(BF16)
    terms = adapter_scale * jnp.dot(
        left, up[...].reshape(held * rank, channels), preferred_element_type=F32
    )
    n = terms.shape[0] // n_msg
    for k in range(n_msg):
        outs[k][...] = terms[k * n : (k + 1) * n]
    rows = DECODE_STEPS * sessions
    sums = jnp.sum(total[:rows, rank:], axis=1, keepdims=True)
    factor = lax.rsqrt(sums / (HEAD_COUNT * HEAD_CHANNELS) + norm_eps)
    inverse[...] = jnp.broadcast_to(factor, inverse.shape)


def norm_kernel(gated, inverse, gain, out):
    rows, channels = gated.shape
    normed = gated[...] * inverse[:, :1] * gain[...].astype(F32)
    out[...] = normed.astype(BF16).reshape(out.shape)


def final_kernel(n_msg, *refs):
    msgs = refs[:n_msg]
    place, inverse, out = refs[n_msg:]
    terms = jnp.concatenate([m[...].astype(F32) for m in msgs], axis=0)
    mine = lax.dot_general(
        place[...], terms, (((0,), (0,)), ((), ())), precision=HIGHEST, preferred_element_type=F32
    )
    out[...] = (mine * inverse[:, :1]).reshape(out.shape)


def vmem():
    return pl.BlockSpec(memory_space=pltpu.VMEM)


def smem():
    return pl.BlockSpec(memory_space=pltpu.SMEM)


def shape(dims, dtype):
    return jax.ShapeDtypeStruct(dims, dtype)


def per_device(
    session_head_state,
    convolved_activation,
    gate_activations,
    state_input_projection,
    state_output_projection,
    raw_step_sizes,
    step_size_bias,
    log_decay_rate,
    skip_coefficient,
    group_norm_gain,
    adapter_down_weight,
    adapter_up_weight,
    adapter_per_session,
    adapter_storage_slot,
):
    sessions, heads, _, state_size = session_head_state.shape
    channels = heads * HEAD_CHANNELS
    rows = DECODE_STEPS * sessions
    batch_count = lax.axis_size("batch")
    tensor_count = lax.axis_size("tensor")
    capacity = max(2, (sessions + batch_count - 1) // batch_count)
    held = adapter_down_weight.shape[0]
    split = batch_count in (2, 4)
    per_owner = DECODE_STEPS * capacity
    targets = batch_count * per_owner
    n_msg = batch_count if split else 1
    chunks = 4
    me = lax.axis_index("batch")
    group = lax.axis_index("tensor") * heads // (HEAD_COUNT // GROUPS)
    ids = jnp.stack([me, group]).astype(jnp.int32)
    gain = group_norm_gain.reshape(1, channels)

    msg_rows = targets // n_msg
    dims = (sessions, heads, batch_count, capacity, held, chunks, split)
    out = pl.pallas_call(
        functools.partial(front_kernel, dims),
        out_shape=[shape((msg_rows, channels + LANES), BF16)] * n_msg
        + [
            shape((rows, channels), F32),
            shape((rows, RANK), F32),
            shape((rows, channels), F32),
            shape((rows, LANES), F32),
            shape((sessions, heads), F32),
            shape((targets, rows), F32),
        ],
        in_specs=[smem()] * 3 + [pl.BlockSpec(memory_space=pl.ANY)] + [vmem()] * 9,
        out_specs=[vmem()] * (n_msg + 6),
        scratch_shapes=[
            pltpu.VMEM(session_head_state.shape, BF16),
            pltpu.SemaphoreType.DMA((chunks,)),
            pltpu.SMEM((batch_count,), jnp.int32),
        ],
        compiler_params=pltpu.CompilerParams(vmem_limit_bytes=24 << 20),
        cost_estimate=pl.CostEstimate(
            flops=2 * 32 * session_head_state.size,
            bytes_accessed=2 * session_head_state.size,
            transcendentals=0,
        ),
        name="front",
    )(
        ids,
        adapter_per_session,
        adapter_storage_slot,
        session_head_state,
        convolved_activation,
        gate_activations,
        state_input_projection,
        state_output_projection,
        raw_step_sizes,
        step_size_bias.reshape(1, heads),
        log_decay_rate.reshape(1, heads),
        skip_coefficient.reshape(1, heads),
        gain,
    )
    msgs = out[:n_msg]
    gated, squares, drive, b_rows, keep, place = out[n_msg:]

    def exchange(blocks):
        if split:
            return [blocks[0]] + [
                lax.ppermute(
                    blocks[k], "batch", [(i, i ^ k) for i in range(batch_count)]
                )
                for k in range(1, batch_count)
            ]
        block = blocks[0].reshape(batch_count, per_owner, -1)
        block = lax.all_to_all(block, "batch", split_axis=0, concat_axis=0, tiled=True)
        return [block.reshape(targets, -1)]

    arrived = exchange(msgs)

    pair = 2
    updated = pl.pallas_call(
        functools.partial(state_kernel, sessions, heads, pair),
        grid=(sessions // pair,),
        out_shape=shape(session_head_state.shape, BF16),
        in_specs=[
            pl.BlockSpec((rows, channels), lambda i: (0, 0)),
            pl.BlockSpec((rows, LANES), lambda i: (0, 0)),
            smem(),
            pl.BlockSpec((pair, heads, HEAD_CHANNELS, state_size), lambda i: (i, 0, 0, 0)),
        ],
        out_specs=pl.BlockSpec((pair, heads, HEAD_CHANNELS, state_size), lambda i: (i, 0, 0, 0)),
        scratch_shapes=[pltpu.VMEM((channels, 2 * rows), BF16)],
        compiler_params=pltpu.CompilerParams(vmem_limit_bytes=16 << 20),
        cost_estimate=pl.CostEstimate(
            flops=8 * session_head_state.size,
            bytes_accessed=4 * session_head_state.size,
            transcendentals=0,
        ),
        name="state",
    )(drive, b_rows, keep, session_head_state)

    partial, pick = pl.pallas_call(
        functools.partial(down_kernel, n_msg),
        out_shape=[shape((targets, 2 * RANK), F32), shape((targets, LANES), F32)],
        in_specs=[vmem()] * (n_msg + 2),
        out_specs=[vmem()] * 2,
        name="down",
    )(*arrived, adapter_down_weight, squares)

    if tensor_count in (2, 4):
        parts = [partial] + [
            lax.ppermute(partial, "tensor", [(i, i ^ k) for i in range(tensor_count)])
            for k in range(1, tensor_count)
        ]
    else:
        parts = [lax.psum(partial, "tensor")]

    out = pl.pallas_call(
        functools.partial(up_kernel, len(parts), n_msg, sessions),
        out_shape=[shape((msg_rows, channels), F32)] * n_msg + [shape((rows, LANES), F32)],
        in_specs=[vmem()] * (len(parts) + 2),
        out_specs=[vmem()] * (n_msg + 1),
        name="up",
    )(*parts, pick, adapter_up_weight)
    terms, inverse = out[:n_msg], out[n_msg]
    returned = exchange(terms)

    normed = pl.pallas_call(
        norm_kernel,
        out_shape=shape((DECODE_STEPS, sessions, channels), BF16),
        in_specs=[vmem()] * 3,
        out_specs=vmem(),
        name="norm",
    )(gated, inverse, gain)

    delta = pl.pallas_call(
        functools.partial(final_kernel, n_msg),
        out_shape=shape((DECODE_STEPS, sessions, channels), F32),
        in_specs=[vmem()] * (n_msg + 2),
        out_specs=vmem(),
        name="final",
    )(*returned, place, inverse)
    return (updated, normed, delta)


def solution(mesh):
    placed = (
        P(("groups", "batch"), "tensor", None, None),
        P(None, ("groups", "batch"), "tensor"),
        P(None, ("groups", "batch"), "tensor"),
        P(None, ("groups", "batch"), None, None),
        P(None, ("groups", "batch"), None, None),
        P(None, ("groups", "batch"), "tensor"),
        P("tensor"),
        P("tensor"),
        P("tensor"),
        P("tensor"),
        P(("groups", "batch"), None, "tensor"),
        P(("groups", "batch"), None, "tensor"),
        P(("groups", "batch")),
        P("groups"),
    )
    return jax.shard_map(
        per_device,
        mesh=mesh,
        in_specs=placed,
        out_specs=(
            P(("groups", "batch"), "tensor", None, None),
            P(None, ("groups", "batch"), "tensor"),
            P(None, ("groups", "batch"), "tensor"),
        ),
        check_vma=False,
    )
```

```python
import functools

import jax
import jax.numpy as jnp
from jax import lax
from jax.experimental import pallas as pl
from jax.experimental.pallas import tpu as pltpu
from jax.sharding import PartitionSpec as P

HEAD_COUNT = 64
HEAD_CHANNELS = 64
GROUPS = 4
DECODE_STEPS = 2
RANK = 64
LANES = 128

adapter_scale = 2.0
norm_eps = 1e-05

F32 = jnp.float32
BF16 = jnp.bfloat16
HIGHEST = lax.Precision.HIGHEST
NT = (((1,), (1,)), ((), ()))


def iota(shape, axis):
    return lax.broadcasted_iota(jnp.int32, shape, axis)


def front_kernel(dims, *refs):
    sessions, heads, batch_count, capacity, adapters_held, chunks, split = dims
    n_msg = batch_count if split else 1
    inputs, refs = refs[:14], refs[14:]
    msgs, refs = refs[:n_msg], refs[n_msg:]
    gated_ref, square_ref, drive_ref, b_ref, keep_ref, place_ref, gain_ref = refs[:7]
    held, down_out, up_out = refs[7:10]
    local, (sems, small_sems, weight_sems, counts) = refs[10:21], refs[21:]
    state, down, up = inputs[:3]
    channels = heads * HEAD_CHANNELS
    rows = DECODE_STEPS * sessions
    part = heads // chunks
    width = part * HEAD_CHANNELS

    loads = [
        pltpu.make_async_copy(source, target, small_sems.at[i])
        for i, (source, target) in enumerate(zip(inputs[3:], local))
    ]
    for load in loads:
        load.start()
    copies = []
    for i in range(chunks):
        window = pl.ds(i * part, part)
        copy = pltpu.make_async_copy(state.at[:, window], held.at[:, window], sems.at[i])
        copy.start()
        copies.append(copy)
    weights = [
        pltpu.make_async_copy(down, down_out, weight_sems.at[0]),
        pltpu.make_async_copy(up, up_out, weight_sems.at[1]),
    ]
    for load in weights:
        load.start()
    adapter, slot_of, x, z, b, c, raw, bias, rate, skip, gain_rows = local
    me = lax.axis_index("batch")
    group = lax.axis_index("tensor") * heads // (HEAD_COUNT // GROUPS)
    for load in loads:
        load.wait()
    gain = jnp.concatenate(
        [gain_rows[i : i + 1].astype(F32) for i in range(channels // LANES)], axis=1
    )
    gain_ref[...] = gain
    for i in range(batch_count):
        counts[i] = 0
    per_owner = DECODE_STEPS * capacity
    targets = batch_count * per_owner
    to = iota((targets, rows), 0)
    source = iota((targets, rows), 1)
    lane_to = iota((targets, LANES), 0)
    place = jnp.zeros((targets, rows), F32)
    pick = jnp.zeros((targets, LANES), F32)
    for s in range(sessions):
        slot = slot_of[adapter[s]]
        owner = slot // adapters_held
        which = (slot - owner * adapters_held).astype(F32)
        earlier = counts[owner]
        counts[owner] = earlier + 1
        relative = (owner ^ me) if split else owner
        first = relative * per_owner + earlier * DECODE_STEPS
        hit = (to - first == source // sessions) & (source % sessions == s)
        place = jnp.where(hit, 1.0, place)
        mine = (lane_to >= first) & (lane_to < first + DECODE_STEPS)
        pick = jnp.where(mine, which, pick)
    place_ref[...] = place
    place_bf = place.astype(BF16)

    def pick_group(ref):
        values = ref[...].astype(F32).reshape(rows, GROUPS, LANES)
        return jnp.sum(jnp.where(iota(values.shape, 1) == group, values, 0.0), axis=1)

    b_rows = pick_group(b)
    c_rows = pick_group(c)
    b_ref[...] = b_rows
    b1, b2 = b_rows[:sessions], b_rows[sessions:]
    c1, c2 = c_rows[:sessions], c_rows[sessions:]
    bc11 = jnp.sum(b1 * c1, axis=1, keepdims=True)
    bc12 = jnp.sum(b1 * c2, axis=1, keepdims=True)
    bc22 = jnp.sum(b2 * c2, axis=1, keepdims=True)

    def softplus(v):
        return jnp.maximum(v, 0.0) + jnp.log1p(jnp.exp(-jnp.abs(v)))

    step1 = softplus(raw[0] + bias[...])
    step2 = softplus(raw[1] + bias[...])
    speed = -jnp.exp(rate[...])
    decay1 = jnp.exp(speed * step1)
    decay2 = jnp.exp(speed * step2)
    keep = decay1 * decay2
    keep_ref[...] = keep
    factors = jnp.concatenate(
        [
            decay1,
            step1 * bc11 + skip[...],
            keep,
            decay2 * step1 * bc12,
            step2 * bc22 + skip[...],
            decay2 * step1,
            step2,
        ],
        axis=0,
    )
    spread = (iota((heads, channels), 1) // HEAD_CHANNELS == iota((heads, channels), 0)).astype(F32)
    wide = jnp.dot(factors, spread, precision=HIGHEST, preferred_element_type=F32)
    wide = [wide[i * sessions : (i + 1) * sessions] for i in range(7)]
    x1 = x[0].astype(F32)
    x2 = x[1].astype(F32)
    drive_ref[...] = jnp.concatenate([wide[5] * x1, wide[6] * x2], axis=0)
    base1 = x1 * wide[1]
    base2 = x1 * wide[3] + x2 * wide[4]
    gates = jnp.concatenate([z[0].astype(F32), z[1].astype(F32)], axis=0)
    gates = gates / (1.0 + jnp.exp(-gates))
    base = jnp.concatenate([base1, base2], axis=0)
    scale = jnp.concatenate([wide[0], wide[2]], axis=0)
    row_session = iota((rows, LANES), 0) % sessions
    c_blocks = jnp.concatenate(
        [jnp.where(row_session == s, c_rows, 0.0).astype(BF16) for s in range(sessions)], axis=1
    )
    squares = jnp.zeros((rows, LANES), F32)
    for i in range(chunks):
        copies[i].wait()
        lanes = slice(i * width, (i + 1) * width)
        block = jnp.concatenate(
            [
                held[s, i * part : (i + 1) * part].reshape(width, LANES)
                for s in range(sessions)
            ],
            axis=1,
        )
        reads = lax.dot_general(c_blocks, block, NT, preferred_element_type=F32)
        gated = (scale[:, lanes] * reads + base[:, lanes]) * gates[:, lanes]
        gated_ref[:, lanes] = gated
        for j in range(width // LANES):
            piece = gated[:, j * LANES : (j + 1) * LANES]
            squares = squares + piece * piece
        weighted = (gated * gain[:, lanes]).astype(BF16)
        packed = jnp.dot(place_bf, weighted, preferred_element_type=F32)
        for k in range(n_msg):
            n = targets // n_msg
            msgs[k][:, lanes] = packed[k * n : (k + 1) * n].astype(BF16)
    for k in range(n_msg):
        n = targets // n_msg
        msgs[k][:, channels:] = pick[k * n : (k + 1) * n].astype(BF16)
    square_ref[...] = squares[:, :RANK] + squares[:, RANK:]
    for load in weights:
        load.wait()


def state_kernel(pair, drive, b, keep, state, out, made, sems):
    sessions, heads, _, _ = state.shape
    rows = DECODE_STEPS * sessions
    turned = drive[...].T
    high = turned.astype(BF16)
    low = (turned - high.astype(F32)).astype(BF16)
    left = jnp.concatenate([high, low], axis=1)
    row_session = iota((rows, LANES), 0) % sessions
    b_rows = b[...]
    copies = []
    for i in range(sessions // pair):
        right = jnp.concatenate(
            [jnp.where(row_session == i * pair + q, b_rows, 0.0) for q in range(pair)], axis=1
        )
        right = jnp.concatenate([right, right], axis=0).astype(BF16)
        for h in range(heads):
            piece = slice(h * HEAD_CHANNELS, (h + 1) * HEAD_CHANNELS)
            added = jnp.dot(left[piece], right, preferred_element_type=F32)
            for q in range(pair):
                s = i * pair + q
                kept = state[s, h].astype(F32) * keep[s, h]
                made[s, h] = (kept + added[:, q * LANES : (q + 1) * LANES]).astype(BF16)
        window = pl.ds(i * pair, pair)
        copy = pltpu.make_async_copy(made.at[window], out.at[window], sems.at[i])
        copy.start()
        copies.append(copy)
    for copy in copies:
        copy.wait()


def down_kernel(n_msg, *refs):
    msgs = refs[:n_msg]
    down, squares, out, pick_ref = refs[n_msg:]
    held, rank, channels = down.shape
    rows = jnp.concatenate([m[...].astype(F32) for m in msgs], axis=0)
    pick = rows[:, channels:]
    weights = down[...].reshape(held * rank, channels)
    ranks = lax.dot_general(
        rows[:, :channels].astype(BF16), weights, NT, preferred_element_type=F32
    )
    chosen = jnp.zeros((rows.shape[0], rank), F32)
    for j in range(held):
        chosen = jnp.where(pick[:, :rank] == j, ranks[:, j * rank : (j + 1) * rank], chosen)
    pick_ref[...] = pick
    n_squares = squares.shape[0]
    if n_squares < chosen.shape[0]:
        filled = jnp.concatenate(
            [squares[...], jnp.zeros((chosen.shape[0] - n_squares, rank), F32)], axis=0
        )
    else:
        filled = squares[...]
    out[...] = jnp.concatenate([chosen, filled], axis=1)


def up_kernel(n_sum, n_msg, sessions, *refs):
    parts = refs[:n_sum]
    pick, up = refs[n_sum : n_sum + 2]
    outs = refs[n_sum + 2 : n_sum + 2 + n_msg]
    inverse = refs[n_sum + 2 + n_msg]
    held, rank, channels = up.shape
    total = parts[0][...]
    for p in parts[1:]:
        total = total + p[...]
    ranks = total[:, :rank]
    left = jnp.concatenate(
        [jnp.where(pick[:, :rank] == j, ranks, 0.0) for j in range(held)], axis=1
    ).astype(BF16)
    terms = adapter_scale * jnp.dot(
        left, up[...].reshape(held * rank, channels), preferred_element_type=F32
    )
    n = terms.shape[0] // n_msg
    for k in range(n_msg):
        outs[k][...] = terms[k * n : (k + 1) * n]
    rows = DECODE_STEPS * sessions
    sums = jnp.sum(total[:rows, rank:], axis=1, keepdims=True)
    factor = lax.rsqrt(sums / (HEAD_COUNT * HEAD_CHANNELS) + norm_eps)
    inverse[...] = jnp.broadcast_to(factor, inverse.shape)


def norm_kernel(gated, inverse, gain, out):
    rows, channels = gated.shape
    normed = gated[...] * inverse[:, :1] * gain[...]
    out[...] = normed.astype(BF16).reshape(out.shape)


def final_kernel(n_msg, *refs):
    msgs = refs[:n_msg]
    place, inverse, out = refs[n_msg:]
    terms = jnp.concatenate([m[...].astype(F32) for m in msgs], axis=0)
    mine = lax.dot_general(
        place[...], terms, (((0,), (0,)), ((), ())), precision=HIGHEST, preferred_element_type=F32
    )
    out[...] = (mine * inverse[:, :1]).reshape(out.shape)


def vmem():
    return pl.BlockSpec(memory_space=pltpu.VMEM)


def smem():
    return pl.BlockSpec(memory_space=pltpu.SMEM)


def shape(dims, dtype):
    return jax.ShapeDtypeStruct(dims, dtype)


def per_device(
    session_head_state,
    convolved_activation,
    gate_activations,
    state_input_projection,
    state_output_projection,
    raw_step_sizes,
    step_size_bias,
    log_decay_rate,
    skip_coefficient,
    group_norm_gain,
    adapter_down_weight,
    adapter_up_weight,
    adapter_per_session,
    adapter_storage_slot,
):
    sessions, heads, _, state_size = session_head_state.shape
    channels = heads * HEAD_CHANNELS
    rows = DECODE_STEPS * sessions
    batch_count = lax.axis_size("batch")
    tensor_count = lax.axis_size("tensor")
    capacity = max(2, (sessions + batch_count - 1) // batch_count)
    adapters_held = adapter_down_weight.shape[0]
    split = batch_count in (2, 4)
    per_owner = DECODE_STEPS * capacity
    targets = batch_count * per_owner
    n_msg = batch_count if split else 1
    chunks = 4
    msg_rows = targets // n_msg
    dims = (sessions, heads, batch_count, capacity, adapters_held, chunks, split)
    smalls = (
        adapter_per_session,
        adapter_storage_slot,
        convolved_activation,
        gate_activations,
        state_input_projection,
        state_output_projection,
        raw_step_sizes,
        step_size_bias.reshape(1, heads),
        log_decay_rate.reshape(1, heads),
        skip_coefficient.reshape(1, heads),
        group_norm_gain.reshape(channels // LANES, LANES),
    )
    out = pl.pallas_call(
        functools.partial(front_kernel, dims),
        out_shape=[shape((msg_rows, channels + LANES), BF16)] * n_msg
        + [
            shape((rows, channels), F32),
            shape((rows, RANK), F32),
            shape((rows, channels), F32),
            shape((rows, LANES), F32),
            shape((sessions, heads), F32),
            shape((targets, rows), F32),
            shape((1, channels), F32),
            shape(session_head_state.shape, BF16),
            shape(adapter_down_weight.shape, BF16),
            shape(adapter_up_weight.shape, BF16),
        ],
        in_specs=[pl.BlockSpec(memory_space=pltpu.HBM)] * 14,
        out_specs=[vmem()] * (n_msg + 10),
        scratch_shapes=[pltpu.SMEM(v.shape, v.dtype) for v in smalls[:2]]
        + [pltpu.VMEM(v.shape, v.dtype) for v in smalls[2:]]
        + [
            pltpu.SemaphoreType.DMA((chunks,)),
            pltpu.SemaphoreType.DMA((len(smalls),)),
            pltpu.SemaphoreType.DMA((2,)),
            pltpu.SMEM((batch_count,), jnp.int32),
        ],
        compiler_params=pltpu.CompilerParams(vmem_limit_bytes=16 << 20),
        cost_estimate=pl.CostEstimate(
            flops=2 * 32 * session_head_state.size,
            bytes_accessed=2 * session_head_state.size,
            transcendentals=0,
        ),
        name="front",
    )(session_head_state, adapter_down_weight, adapter_up_weight, *smalls)
    msgs = out[:n_msg]
    gated, squares, drive, b_rows, keep, place, gain, held_state, down, up = out[n_msg:]

    def exchange(blocks):
        if split:
            return [blocks[0]] + [
                lax.ppermute(
                    blocks[k], "batch", [(i, i ^ k) for i in range(batch_count)]
                )
                for k in range(1, batch_count)
            ]
        block = blocks[0].reshape(batch_count, per_owner, -1)
        block = lax.all_to_all(block, "batch", split_axis=0, concat_axis=0, tiled=True)
        return [block.reshape(targets, -1)]

    arrived = exchange(msgs)

    pair = 2
    updated = pl.pallas_call(
        functools.partial(state_kernel, pair),
        out_shape=shape(session_head_state.shape, BF16),
        in_specs=[vmem(), vmem(), smem(), vmem()],
        out_specs=pl.BlockSpec(memory_space=pltpu.HBM),
        scratch_shapes=[
            pltpu.VMEM(session_head_state.shape, BF16),
            pltpu.SemaphoreType.DMA((sessions // pair,)),
        ],
        compiler_params=pltpu.CompilerParams(vmem_limit_bytes=12 << 20),
        cost_estimate=pl.CostEstimate(
            flops=8 * session_head_state.size,
            bytes_accessed=4 * session_head_state.size,
            transcendentals=0,
        ),
        name="state",
    )(drive, b_rows, keep, held_state)
    arrived = lax.optimization_barrier((arrived, updated))[0]

    partial, pick = pl.pallas_call(
        functools.partial(down_kernel, n_msg),
        out_shape=[shape((targets, 2 * RANK), F32), shape((targets, LANES), F32)],
        in_specs=[vmem()] * (n_msg + 2),
        out_specs=[vmem()] * 2,
        compiler_params=pltpu.CompilerParams(vmem_limit_bytes=4 << 20),
        name="down",
    )(*arrived, down, squares)

    if tensor_count in (2, 4):
        parts = [partial] + [
            lax.ppermute(partial, "tensor", [(i, i ^ k) for i in range(tensor_count)])
            for k in range(1, tensor_count)
        ]
    else:
        parts = [lax.psum(partial, "tensor")]

    out = pl.pallas_call(
        functools.partial(up_kernel, len(parts), n_msg, sessions),
        out_shape=[shape((msg_rows, channels), F32)] * n_msg + [shape((rows, LANES), F32)],
        in_specs=[vmem()] * (len(parts) + 2),
        out_specs=[vmem()] * (n_msg + 1),
        compiler_params=pltpu.CompilerParams(vmem_limit_bytes=4 << 20),
        name="up",
    )(*parts, pick, up)
    terms, inverse = out[:n_msg], out[n_msg]
    returned = exchange(terms)

    normed = pl.pallas_call(
        norm_kernel,
        out_shape=shape((DECODE_STEPS, sessions, channels), BF16),
        in_specs=[vmem()] * 3,
        out_specs=vmem(),
        compiler_params=pltpu.CompilerParams(vmem_limit_bytes=4 << 20),
        name="norm",
    )(gated, inverse, gain)

    delta = pl.pallas_call(
        functools.partial(final_kernel, n_msg),
        out_shape=shape((DECODE_STEPS, sessions, channels), F32),
        in_specs=[vmem()] * (n_msg + 2),
        out_specs=vmem(),
        compiler_params=pltpu.CompilerParams(vmem_limit_bytes=4 << 20),
        name="final",
    )(*returned, place, inverse)
    return (updated, normed, delta)


def solution(mesh):
    placed = (
        P(("groups", "batch"), "tensor", None, None),
        P(None, ("groups", "batch"), "tensor"),
        P(None, ("groups", "batch"), "tensor"),
        P(None, ("groups", "batch"), None, None),
        P(None, ("groups", "batch"), None, None),
        P(None, ("groups", "batch"), "tensor"),
        P("tensor"),
        P("tensor"),
        P("tensor"),
        P("tensor"),
        P(("groups", "batch"), None, "tensor"),
        P(("groups", "batch"), None, "tensor"),
        P(("groups", "batch")),
        P("groups"),
    )
    return jax.shard_map(
        per_device,
        mesh=mesh,
        in_specs=placed,
        out_specs=(
            P(("groups", "batch"), "tensor", None, None),
            P(None, ("groups", "batch"), "tensor"),
            P(None, ("groups", "batch"), "tensor"),
        ),
        check_vma=False,
    )
```

```python
import functools

import jax
import jax.numpy as jnp
from jax import lax
from jax.experimental import pallas as pl
from jax.experimental.pallas import tpu as pltpu
from jax.sharding import PartitionSpec as P

HEAD_COUNT = 64
HEAD_CHANNELS = 64
GROUPS = 4
DECODE_STEPS = 2
RANK = 64
LANES = 128

adapter_scale = 2.0
norm_eps = 1e-05

F32 = jnp.float32
BF16 = jnp.bfloat16
HIGHEST = lax.Precision.HIGHEST
NT = (((1,), (1,)), ((), ()))


def iota(shape, axis):
    return lax.broadcasted_iota(jnp.int32, shape, axis)


def front_kernel(dims, *refs):
    sessions, heads, batch_count, capacity, adapters_held, chunks, split = dims
    n_msg = batch_count if split else 1
    inputs, refs = refs[:14], refs[14:]
    msgs, refs = refs[:n_msg], refs[n_msg:]
    gated_ref, square_ref, drive_ref, b_ref, keep_ref, place_ref, gain_ref = refs[:7]
    held, down_out, up_out = refs[7:10]
    local, (sems, small_sems, weight_sems, counts) = refs[10:21], refs[21:]
    state, down, up = inputs[:3]
    channels = heads * HEAD_CHANNELS
    rows = DECODE_STEPS * sessions
    part = heads // chunks
    width = part * HEAD_CHANNELS

    loads = [
        pltpu.make_async_copy(source, target, small_sems.at[i])
        for i, (source, target) in enumerate(zip(inputs[3:], local))
    ]
    for load in loads:
        load.start()
    copies = []
    for i in range(chunks):
        window = pl.ds(i * part, part)
        copy = pltpu.make_async_copy(state.at[:, window], held.at[:, window], sems.at[i])
        copy.start()
        copies.append(copy)
    weights = [
        pltpu.make_async_copy(down, down_out, weight_sems.at[0]),
        pltpu.make_async_copy(up, up_out, weight_sems.at[1]),
    ]
    for load in weights:
        load.start()
    adapter, slot_of, x, z, b, c, raw, bias, rate, skip, gain_rows = local
    me = lax.axis_index("batch")
    group = lax.axis_index("tensor") * heads // (HEAD_COUNT // GROUPS)
    for load in loads:
        load.wait()
    gain = jnp.concatenate(
        [gain_rows[i : i + 1].astype(F32) for i in range(channels // LANES)], axis=1
    )
    gain_ref[...] = gain
    for i in range(batch_count):
        counts[i] = 0
    per_owner = DECODE_STEPS * capacity
    targets = batch_count * per_owner
    to = iota((targets, rows), 0)
    source = iota((targets, rows), 1)
    lane_to = iota((targets, LANES), 0)
    place = jnp.zeros((targets, rows), F32)
    pick = jnp.zeros((targets, LANES), F32)
    for s in range(sessions):
        slot = slot_of[adapter[s]]
        owner = slot // adapters_held
        which = (slot - owner * adapters_held).astype(F32)
        earlier = counts[owner]
        counts[owner] = earlier + 1
        relative = (owner ^ me) if split else owner
        first = relative * per_owner + earlier * DECODE_STEPS
        hit = (to - first == source // sessions) & (source % sessions == s)
        place = jnp.where(hit, 1.0, place)
        mine = (lane_to >= first) & (lane_to < first + DECODE_STEPS)
        pick = jnp.where(mine, which, pick)
    place_ref[...] = place
    place_bf = place.astype(BF16)

    def pick_group(ref):
        values = ref[...].astype(F32).reshape(rows, GROUPS, LANES)
        return jnp.sum(jnp.where(iota(values.shape, 1) == group, values, 0.0), axis=1)

    b_rows = pick_group(b)
    c_rows = pick_group(c)
    b_ref[...] = b_rows
    b1, b2 = b_rows[:sessions], b_rows[sessions:]
    c1, c2 = c_rows[:sessions], c_rows[sessions:]
    bc11 = jnp.sum(b1 * c1, axis=1, keepdims=True)
    bc12 = jnp.sum(b1 * c2, axis=1, keepdims=True)
    bc22 = jnp.sum(b2 * c2, axis=1, keepdims=True)

    def softplus(v):
        return jnp.maximum(v, 0.0) + jnp.log1p(jnp.exp(-jnp.abs(v)))

    step1 = softplus(raw[0] + bias[...])
    step2 = softplus(raw[1] + bias[...])
    speed = -jnp.exp(rate[...])
    decay1 = jnp.exp(speed * step1)
    decay2 = jnp.exp(speed * step2)
    keep = decay1 * decay2
    keep_ref[...] = keep
    factors = jnp.concatenate(
        [
            decay1,
            step1 * bc11 + skip[...],
            keep,
            decay2 * step1 * bc12,
            step2 * bc22 + skip[...],
            decay2 * step1,
            step2,
        ],
        axis=0,
    )
    spread = (iota((heads, channels), 1) // HEAD_CHANNELS == iota((heads, channels), 0)).astype(F32)
    wide = jnp.dot(factors, spread, precision=HIGHEST, preferred_element_type=F32)
    wide = [wide[i * sessions : (i + 1) * sessions] for i in range(7)]
    x1 = x[0].astype(F32)
    x2 = x[1].astype(F32)
    drive_ref[...] = jnp.concatenate([wide[5] * x1, wide[6] * x2], axis=0)
    base1 = x1 * wide[1]
    base2 = x1 * wide[3] + x2 * wide[4]
    gates = jnp.concatenate([z[0].astype(F32), z[1].astype(F32)], axis=0)
    gates = gates / (1.0 + jnp.exp(-gates))
    base = jnp.concatenate([base1, base2], axis=0)
    scale = jnp.concatenate([wide[0], wide[2]], axis=0)
    row_session = iota((rows, LANES), 0) % sessions
    c_blocks = jnp.concatenate(
        [jnp.where(row_session == s, c_rows, 0.0).astype(BF16) for s in range(sessions)], axis=1
    )
    squares = jnp.zeros((rows, LANES), F32)
    for i in range(chunks):
        copies[i].wait()
        lanes = slice(i * width, (i + 1) * width)
        block = jnp.concatenate(
            [
                held[s, i * part : (i + 1) * part].reshape(width, LANES)
                for s in range(sessions)
            ],
            axis=1,
        )
        reads = lax.dot_general(c_blocks, block, NT, preferred_element_type=F32)
        gated = (scale[:, lanes] * reads + base[:, lanes]) * gates[:, lanes]
        gated_ref[:, lanes] = gated
        for j in range(width // LANES):
            piece = gated[:, j * LANES : (j + 1) * LANES]
            squares = squares + piece * piece
        weighted = (gated * gain[:, lanes]).astype(BF16)
        packed = jnp.dot(place_bf, weighted, preferred_element_type=F32)
        for k in range(n_msg):
            n = targets // n_msg
            msgs[k][:, lanes] = packed[k * n : (k + 1) * n].astype(BF16)
    for k in range(n_msg):
        n = targets // n_msg
        msgs[k][:, channels:] = pick[k * n : (k + 1) * n].astype(BF16)
    square_ref[...] = squares[:, :RANK] + squares[:, RANK:]
    for load in weights:
        load.wait()


def state_kernel(pair, drive, b, keep, state, out, made, sems):
    sessions, heads, _, _ = state.shape
    rows = DECODE_STEPS * sessions
    turned = drive[...].T
    high = turned.astype(BF16)
    low = (turned - high.astype(F32)).astype(BF16)
    left = jnp.concatenate([high, low], axis=1)
    row_session = iota((rows, LANES), 0) % sessions
    b_rows = b[...]
    copies = []
    for i in range(sessions // pair):
        right = jnp.concatenate(
            [jnp.where(row_session == i * pair + q, b_rows, 0.0) for q in range(pair)], axis=1
        )
        right = jnp.concatenate([right, right], axis=0).astype(BF16)
        for h in range(heads):
            piece = slice(h * HEAD_CHANNELS, (h + 1) * HEAD_CHANNELS)
            added = jnp.dot(left[piece], right, preferred_element_type=F32)
            for q in range(pair):
                s = i * pair + q
                kept = state[s, h].astype(F32) * keep[s, h]
                made[s, h] = (kept + added[:, q * LANES : (q + 1) * LANES]).astype(BF16)
        window = pl.ds(i * pair, pair)
        copy = pltpu.make_async_copy(made.at[window], out.at[window], sems.at[i])
        copy.start()
        copies.append(copy)
    for copy in copies:
        copy.wait()


def down_kernel(n_msg, *refs):
    msgs = refs[:n_msg]
    down, squares, out, pick_ref = refs[n_msg:]
    held, rank, channels = down.shape
    rows = jnp.concatenate([m[...].astype(F32) for m in msgs], axis=0)
    pick = rows[:, channels:]
    weights = down[...].reshape(held * rank, channels)
    ranks = lax.dot_general(
        rows[:, :channels].astype(BF16), weights, NT, preferred_element_type=F32
    )
    chosen = jnp.zeros((rows.shape[0], rank), F32)
    for j in range(held):
        chosen = jnp.where(pick[:, :rank] == j, ranks[:, j * rank : (j + 1) * rank], chosen)
    pick_ref[...] = pick
    n_squares = squares.shape[0]
    if n_squares < chosen.shape[0]:
        filled = jnp.concatenate(
            [squares[...], jnp.zeros((chosen.shape[0] - n_squares, rank), F32)], axis=0
        )
    else:
        filled = squares[...]
    out[...] = jnp.concatenate([chosen, filled], axis=1)


def up_kernel(n_sum, n_msg, sessions, *refs):
    parts = refs[:n_sum]
    pick, up = refs[n_sum : n_sum + 2]
    outs = refs[n_sum + 2 : n_sum + 2 + n_msg]
    inverse = refs[n_sum + 2 + n_msg]
    held, rank, channels = up.shape
    total = parts[0][...]
    for p in parts[1:]:
        total = total + p[...]
    ranks = total[:, :rank]
    left = jnp.concatenate(
        [jnp.where(pick[:, :rank] == j, ranks, 0.0) for j in range(held)], axis=1
    ).astype(BF16)
    terms = adapter_scale * jnp.dot(
        left, up[...].reshape(held * rank, channels), preferred_element_type=F32
    )
    n = terms.shape[0] // n_msg
    for k in range(n_msg):
        outs[k][...] = terms[k * n : (k + 1) * n]
    rows = DECODE_STEPS * sessions
    sums = jnp.sum(total[:rows, rank:], axis=1, keepdims=True)
    factor = lax.rsqrt(sums / (HEAD_COUNT * HEAD_CHANNELS) + norm_eps)
    inverse[...] = jnp.broadcast_to(factor, inverse.shape)


def norm_kernel(gated, inverse, gain, out):
    rows, channels = gated.shape
    normed = gated[...] * inverse[:, :1] * gain[...]
    out[...] = normed.astype(BF16).reshape(out.shape)


def final_kernel(n_msg, *refs):
    msgs = refs[:n_msg]
    place, inverse, out = refs[n_msg:]
    terms = jnp.concatenate([m[...].astype(F32) for m in msgs], axis=0)
    mine = lax.dot_general(
        place[...], terms, (((0,), (0,)), ((), ())), precision=HIGHEST, preferred_element_type=F32
    )
    out[...] = (mine * inverse[:, :1]).reshape(out.shape)


def vmem():
    return pl.BlockSpec(memory_space=pltpu.VMEM)


def smem():
    return pl.BlockSpec(memory_space=pltpu.SMEM)


def shape(dims, dtype):
    return jax.ShapeDtypeStruct(dims, dtype)


def per_device(
    session_head_state,
    convolved_activation,
    gate_activations,
    state_input_projection,
    state_output_projection,
    raw_step_sizes,
    step_size_bias,
    log_decay_rate,
    skip_coefficient,
    group_norm_gain,
    adapter_down_weight,
    adapter_up_weight,
    adapter_per_session,
    adapter_storage_slot,
):
    sessions, heads, _, state_size = session_head_state.shape
    channels = heads * HEAD_CHANNELS
    rows = DECODE_STEPS * sessions
    batch_count = lax.axis_size("batch")
    tensor_count = lax.axis_size("tensor")
    capacity = max(2, (sessions + batch_count - 1) // batch_count)
    adapters_held = adapter_down_weight.shape[0]
    split = batch_count in (2, 4)
    per_owner = DECODE_STEPS * capacity
    targets = batch_count * per_owner
    n_msg = batch_count if split else 1
    chunks = 4
    msg_rows = targets // n_msg
    dims = (sessions, heads, batch_count, capacity, adapters_held, chunks, split)
    smalls = (
        adapter_per_session,
        adapter_storage_slot,
        convolved_activation,
        gate_activations,
        state_input_projection,
        state_output_projection,
        raw_step_sizes,
        step_size_bias.reshape(1, heads),
        log_decay_rate.reshape(1, heads),
        skip_coefficient.reshape(1, heads),
        group_norm_gain.reshape(channels // LANES, LANES),
    )
    out = pl.pallas_call(
        functools.partial(front_kernel, dims),
        out_shape=[shape((msg_rows, channels + LANES), BF16)] * n_msg
        + [
            shape((rows, channels), F32),
            shape((rows, RANK), F32),
            shape((rows, channels), F32),
            shape((rows, LANES), F32),
            shape((sessions, heads), F32),
            shape((targets, rows), F32),
            shape((1, channels), F32),
            shape(session_head_state.shape, BF16),
            shape(adapter_down_weight.shape, BF16),
            shape(adapter_up_weight.shape, BF16),
        ],
        in_specs=[pl.BlockSpec(memory_space=pltpu.HBM)] * 14,
        out_specs=[vmem()] * (n_msg + 10),
        scratch_shapes=[pltpu.SMEM(v.shape, v.dtype) for v in smalls[:2]]
        + [pltpu.VMEM(v.shape, v.dtype) for v in smalls[2:]]
        + [
            pltpu.SemaphoreType.DMA((chunks,)),
            pltpu.SemaphoreType.DMA((len(smalls),)),
            pltpu.SemaphoreType.DMA((2,)),
            pltpu.SMEM((batch_count,), jnp.int32),
        ],
        compiler_params=pltpu.CompilerParams(vmem_limit_bytes=16 << 20),
        cost_estimate=pl.CostEstimate(
            flops=2 * 32 * session_head_state.size,
            bytes_accessed=2 * session_head_state.size,
            transcendentals=0,
        ),
        name="front",
    )(*[pltpu.with_memory_space_constraint(v, pltpu.HBM) for v in (session_head_state, adapter_down_weight, adapter_up_weight, *smalls)])
    msgs = out[:n_msg]
    gated, squares, drive, b_rows, keep, place, gain, held_state, down, up = out[n_msg:]

    def exchange(blocks):
        if split:
            return [blocks[0]] + [
                lax.ppermute(
                    blocks[k], "batch", [(i, i ^ k) for i in range(batch_count)]
                )
                for k in range(1, batch_count)
            ]
        block = blocks[0].reshape(batch_count, per_owner, -1)
        block = lax.all_to_all(block, "batch", split_axis=0, concat_axis=0, tiled=True)
        return [block.reshape(targets, -1)]

    arrived = exchange(msgs)

    pair = 2
    updated = pl.pallas_call(
        functools.partial(state_kernel, pair),
        out_shape=shape(session_head_state.shape, BF16),
        in_specs=[vmem(), vmem(), smem(), vmem()],
        out_specs=pl.BlockSpec(memory_space=pltpu.HBM),
        scratch_shapes=[
            pltpu.VMEM(session_head_state.shape, BF16),
            pltpu.SemaphoreType.DMA((sessions // pair,)),
        ],
        compiler_params=pltpu.CompilerParams(vmem_limit_bytes=12 << 20),
        cost_estimate=pl.CostEstimate(
            flops=8 * session_head_state.size,
            bytes_accessed=4 * session_head_state.size,
            transcendentals=0,
        ),
        name="state",
    )(drive, b_rows, keep, held_state)
    arrived = lax.optimization_barrier((arrived, updated))[0]

    partial, pick = pl.pallas_call(
        functools.partial(down_kernel, n_msg),
        out_shape=[shape((targets, 2 * RANK), F32), shape((targets, LANES), F32)],
        in_specs=[vmem()] * (n_msg + 2),
        out_specs=[vmem()] * 2,
        compiler_params=pltpu.CompilerParams(vmem_limit_bytes=4 << 20),
        name="down",
    )(*arrived, down, squares)

    if tensor_count in (2, 4):
        parts = [partial] + [
            lax.ppermute(partial, "tensor", [(i, i ^ k) for i in range(tensor_count)])
            for k in range(1, tensor_count)
        ]
    else:
        parts = [lax.psum(partial, "tensor")]

    out = pl.pallas_call(
        functools.partial(up_kernel, len(parts), n_msg, sessions),
        out_shape=[shape((msg_rows, channels), F32)] * n_msg + [shape((rows, LANES), F32)],
        in_specs=[vmem()] * (len(parts) + 2),
        out_specs=[vmem()] * (n_msg + 1),
        compiler_params=pltpu.CompilerParams(vmem_limit_bytes=4 << 20),
        name="up",
    )(*parts, pick, up)
    terms, inverse = out[:n_msg], out[n_msg]
    returned = exchange(terms)

    normed = pl.pallas_call(
        norm_kernel,
        out_shape=shape((DECODE_STEPS, sessions, channels), BF16),
        in_specs=[vmem()] * 3,
        out_specs=vmem(),
        compiler_params=pltpu.CompilerParams(vmem_limit_bytes=4 << 20),
        name="norm",
    )(gated, inverse, gain)

    delta = pl.pallas_call(
        functools.partial(final_kernel, n_msg),
        out_shape=shape((DECODE_STEPS, sessions, channels), F32),
        in_specs=[vmem()] * (n_msg + 2),
        out_specs=vmem(),
        compiler_params=pltpu.CompilerParams(vmem_limit_bytes=4 << 20),
        name="final",
    )(*returned, place, inverse)
    return (updated, normed, delta)


def solution(mesh):
    placed = (
        P(("groups", "batch"), "tensor", None, None),
        P(None, ("groups", "batch"), "tensor"),
        P(None, ("groups", "batch"), "tensor"),
        P(None, ("groups", "batch"), None, None),
        P(None, ("groups", "batch"), None, None),
        P(None, ("groups", "batch"), "tensor"),
        P("tensor"),
        P("tensor"),
        P("tensor"),
        P("tensor"),
        P(("groups", "batch"), None, "tensor"),
        P(("groups", "batch"), None, "tensor"),
        P(("groups", "batch")),
        P("groups"),
    )
    return jax.shard_map(
        per_device,
        mesh=mesh,
        in_specs=placed,
        out_specs=(
            P(("groups", "batch"), "tensor", None, None),
            P(None, ("groups", "batch"), "tensor"),
            P(None, ("groups", "batch"), "tensor"),
        ),
        check_vma=False,
    )
```

```python
import functools

import jax
import jax.numpy as jnp
from jax import lax
from jax.experimental import pallas as pl
from jax.experimental.pallas import tpu as pltpu
from jax.sharding import PartitionSpec as P

HEAD_COUNT = 64
HEAD_CHANNELS = 64
GROUPS = 4
DECODE_STEPS = 2
RANK = 64
LANES = 128

adapter_scale = 2.0
norm_eps = 1e-05

F32 = jnp.float32
BF16 = jnp.bfloat16
HIGHEST = lax.Precision.HIGHEST
NT = (((1,), (1,)), ((), ()))


def iota(shape, axis):
    return lax.broadcasted_iota(jnp.int32, shape, axis)


def thirds(v):
    high = v.astype(BF16)
    rest = v - high.astype(F32)
    middle = rest.astype(BF16)
    return [high, middle, (rest - middle.astype(F32)).astype(BF16)]


def front_kernel(dims, *refs):
    sessions, heads, batch_count, capacity, adapters_held, chunks, split = dims
    n_msg = batch_count if split else 1
    inputs, refs = refs[:12], refs[12:]
    msgs, refs = refs[:n_msg], refs[n_msg:]
    gated_ref, square_ref, drive_ref, b_ref, keep_ref, place_ref, gain_ref = refs[:7]
    held = refs[7]
    local, (sems, small_sems, counts) = refs[8:19], refs[19:]
    state = inputs[0]
    channels = heads * HEAD_CHANNELS
    rows = DECODE_STEPS * sessions
    part = sessions // chunks

    loads = [
        pltpu.make_async_copy(source, target, small_sems.at[i])
        for i, (source, target) in enumerate(zip(inputs[1:], local))
    ]
    for load in loads:
        load.start()
    copies = []
    for i in range(chunks):
        window = pl.ds(i * part, part)
        copy = pltpu.make_async_copy(state.at[window], held.at[window], sems.at[i])
        copy.start()
        copies.append(copy)
    adapter, slot_of, x, z, b, c, raw, bias, rate, skip, gain_rows = local
    me = lax.axis_index("batch")
    group = lax.axis_index("tensor") * heads // (HEAD_COUNT // GROUPS)
    for load in loads:
        load.wait()
    def pick_group(ref):
        values = ref[...].astype(F32).reshape(rows, GROUPS, LANES)
        return jnp.sum(jnp.where(iota(values.shape, 1) == group, values, 0.0), axis=1)

    b_rows = pick_group(b)
    c_rows = pick_group(c)
    b_ref[...] = b_rows
    row_session = iota((rows, LANES), 0) % sessions
    c_blocks = jnp.concatenate(
        [jnp.where(row_session == s, c_rows, 0.0).astype(BF16) for s in range(sessions)], axis=1
    )
    def read(i):
        copies[i].wait()
        lanes = slice(i * part * LANES, (i + 1) * part * LANES)
        block = jnp.concatenate(
            [held[i * part + s].reshape(channels, LANES) for s in range(part)], axis=1
        )
        return lax.dot_general(c_blocks[:, lanes], block, NT, preferred_element_type=F32)

    reads = read(0)
    b1, b2 = b_rows[:sessions], b_rows[sessions:]
    c1, c2 = c_rows[:sessions], c_rows[sessions:]
    bc11 = jnp.sum(b1 * c1, axis=1, keepdims=True)
    bc12 = jnp.sum(b1 * c2, axis=1, keepdims=True)
    bc22 = jnp.sum(b2 * c2, axis=1, keepdims=True)

    def softplus(v):
        return jnp.maximum(v, 0.0) + jnp.log1p(jnp.exp(-jnp.abs(v)))

    step1 = softplus(raw[0] + bias[...])
    step2 = softplus(raw[1] + bias[...])
    speed = -jnp.exp(rate[...])
    decay1 = jnp.exp(speed * step1)
    decay2 = jnp.exp(speed * step2)
    keep = decay1 * decay2
    keep_ref[...] = keep
    factors = jnp.concatenate(
        [
            decay1,
            step1 * bc11 + skip[...],
            keep,
            decay2 * step1 * bc12,
            step2 * bc22 + skip[...],
            decay2 * step1,
            step2,
        ],
        axis=0,
    )
    reads = reads + read(1)
    gain = jnp.concatenate(
        [gain_rows[i : i + 1].astype(F32) for i in range(channels // LANES)], axis=1
    )
    gain_ref[...] = gain
    spread = (iota((heads, channels), 1) // HEAD_CHANNELS == iota((heads, channels), 0)).astype(F32)
    wide = jnp.dot(
        jnp.concatenate(thirds(factors), axis=1),
        jnp.concatenate([spread] * 3, axis=0).astype(BF16),
        preferred_element_type=F32,
    )
    wide = [wide[i * sessions : (i + 1) * sessions] for i in range(7)]
    x1 = x[0].astype(F32)
    x2 = x[1].astype(F32)
    drive = jnp.concatenate([wide[5] * x1, wide[6] * x2], axis=0)
    base1 = x1 * wide[1]
    base2 = x1 * wide[3] + x2 * wide[4]
    gates = jnp.concatenate([z[0].astype(F32), z[1].astype(F32)], axis=0)
    gates = gates / (1.0 + jnp.exp(-gates))
    base = jnp.concatenate([base1, base2], axis=0)
    scale = jnp.concatenate([wide[0], wide[2]], axis=0)
    reads = reads + read(2)
    high = drive.astype(BF16)
    low = (drive - high.astype(F32)).astype(BF16)
    drive_ref[...] = jnp.concatenate([high, low], axis=0).T
    for i in range(batch_count):
        counts[i] = 0
    per_owner = DECODE_STEPS * capacity
    targets = batch_count * per_owner
    to = iota((targets, rows), 0)
    source = iota((targets, rows), 1)
    lane_to = iota((targets, LANES), 0)
    place = jnp.zeros((targets, rows), F32)
    pick = jnp.zeros((targets, LANES), F32)
    for s in range(sessions):
        slot = slot_of[adapter[s]]
        owner = slot // adapters_held
        which = (slot - owner * adapters_held).astype(F32)
        earlier = counts[owner]
        counts[owner] = earlier + 1
        relative = (owner ^ me) if split else owner
        first = relative * per_owner + earlier * DECODE_STEPS
        hit = (to - first == source // sessions) & (source % sessions == s)
        place = jnp.where(hit, 1.0, place)
        mine = (lane_to >= first) & (lane_to < first + DECODE_STEPS)
        pick = jnp.where(mine, which, pick)
    place_ref[...] = place
    place_bf = place.astype(BF16)

    reads = reads + read(3)
    gated = (scale * reads + base) * gates
    gated_ref[...] = gated
    squares = jnp.zeros((rows, LANES), F32)
    for j in range(channels // LANES):
        piece = gated[:, j * LANES : (j + 1) * LANES]
        squares = squares + piece * piece
    weighted = (gated * gain).astype(BF16)
    packed = jnp.dot(place_bf, weighted, preferred_element_type=F32)
    for k in range(n_msg):
        n = targets // n_msg
        msgs[k][:, :channels] = packed[k * n : (k + 1) * n].astype(BF16)
    for k in range(n_msg):
        n = targets // n_msg
        msgs[k][:, channels:] = pick[k * n : (k + 1) * n].astype(BF16)
    square_ref[...] = squares[:, :RANK] + squares[:, RANK:]


def state_kernel(pair, left, b, keep, state, out):
    sessions, heads = state.shape[:2]
    rows = b.shape[0]
    row_session = iota((rows, LANES), 0) % sessions
    b_rows = b[...]
    for start in range(0, sessions, pair):
        right = jnp.concatenate(
            [jnp.where(row_session == start + q, b_rows, 0.0) for q in range(pair)], axis=1
        )
        right = jnp.concatenate([right, right], axis=0).astype(BF16)
        for h in range(heads):
            piece = slice(h * HEAD_CHANNELS, (h + 1) * HEAD_CHANNELS)
            added = jnp.dot(left[piece], right, preferred_element_type=F32)
            for q in range(pair):
                kept = state[start + q, h].astype(F32) * keep[start + q, h]
                out[start + q, h] = (kept + added[:, q * LANES : (q + 1) * LANES]).astype(BF16)


def norm_kernel(gated, inverse, gain, out):
    normed = gated[...] * inverse[:, :1] * gain[...]
    out[...] = normed.astype(BF16).reshape(out.shape)


def down_kernel(n_msg, *refs):
    msgs = refs[:n_msg]
    down, squares, out, pick_ref = refs[n_msg:]
    held, rank, channels = down.shape
    rows = jnp.concatenate([m[...].astype(F32) for m in msgs], axis=0)
    pick = rows[:, channels:]
    weights = down[...].reshape(held * rank, channels)
    ranks = lax.dot_general(
        rows[:, :channels].astype(BF16), weights, NT, preferred_element_type=F32
    )
    chosen = jnp.zeros((rows.shape[0], rank), F32)
    for j in range(held):
        chosen = jnp.where(pick[:, :rank] == j, ranks[:, j * rank : (j + 1) * rank], chosen)
    pick_ref[...] = pick
    n_squares = squares.shape[0]
    if n_squares < chosen.shape[0]:
        filled = jnp.concatenate(
            [squares[...], jnp.zeros((chosen.shape[0] - n_squares, rank), F32)], axis=0
        )
    else:
        filled = squares[...]
    out[...] = jnp.concatenate([chosen, filled], axis=1)


def up_kernel(n_sum, n_msg, sessions, *refs):
    parts = refs[:n_sum]
    pick, up = refs[n_sum : n_sum + 2]
    outs = refs[n_sum + 2 : n_sum + 2 + n_msg]
    inverse = refs[n_sum + 2 + n_msg]
    held, rank, channels = up.shape
    total = parts[0][...]
    for p in parts[1:]:
        total = total + p[...]
    ranks = total[:, :rank]
    left = jnp.concatenate(
        [jnp.where(pick[:, :rank] == j, ranks, 0.0) for j in range(held)], axis=1
    ).astype(BF16)
    terms = adapter_scale * jnp.dot(
        left, up[...].reshape(held * rank, channels), preferred_element_type=F32
    )
    n = terms.shape[0] // n_msg
    for k in range(n_msg):
        outs[k][...] = terms[k * n : (k + 1) * n]
    rows = DECODE_STEPS * sessions
    sums = jnp.sum(total[:rows, rank:], axis=1, keepdims=True)
    factor = lax.rsqrt(sums / (HEAD_COUNT * HEAD_CHANNELS) + norm_eps)
    inverse[...] = jnp.broadcast_to(factor, inverse.shape)


def final_kernel(n_msg, *refs):
    msgs = refs[:n_msg]
    place, inverse, out = refs[n_msg:]
    terms = jnp.concatenate([m[...] for m in msgs], axis=0)
    one_hot = place[...].astype(BF16)
    mine = lax.dot_general(
        jnp.concatenate([one_hot] * 3, axis=0),
        jnp.concatenate(thirds(terms), axis=0),
        (((0,), (0,)), ((), ())),
        preferred_element_type=F32,
    )
    out[...] = (mine * inverse[:, :1]).reshape(out.shape)


def vmem():
    return pl.BlockSpec(memory_space=pltpu.VMEM)


def smem():
    return pl.BlockSpec(memory_space=pltpu.SMEM)


def shape(dims, dtype):
    return jax.ShapeDtypeStruct(dims, dtype)


def per_device(
    session_head_state,
    convolved_activation,
    gate_activations,
    state_input_projection,
    state_output_projection,
    raw_step_sizes,
    step_size_bias,
    log_decay_rate,
    skip_coefficient,
    group_norm_gain,
    adapter_down_weight,
    adapter_up_weight,
    adapter_per_session,
    adapter_storage_slot,
):
    sessions, heads, _, state_size = session_head_state.shape
    channels = heads * HEAD_CHANNELS
    rows = DECODE_STEPS * sessions
    batch_count = lax.axis_size("batch")
    tensor_count = lax.axis_size("tensor")
    capacity = max(2, (sessions + batch_count - 1) // batch_count)
    adapters_held = adapter_down_weight.shape[0]
    split = batch_count in (2, 4)
    per_owner = DECODE_STEPS * capacity
    targets = batch_count * per_owner
    n_msg = batch_count if split else 1
    chunks = 4
    msg_rows = targets // n_msg
    dims = (sessions, heads, batch_count, capacity, adapters_held, chunks, split)
    smalls = (
        adapter_per_session,
        adapter_storage_slot,
        convolved_activation,
        gate_activations,
        state_input_projection,
        state_output_projection,
        raw_step_sizes,
        step_size_bias.reshape(1, heads),
        log_decay_rate.reshape(1, heads),
        skip_coefficient.reshape(1, heads),
        group_norm_gain.reshape(channels // LANES, LANES),
    )
    out = pl.pallas_call(
        functools.partial(front_kernel, dims),
        out_shape=[shape((msg_rows, channels + LANES), BF16)] * n_msg
        + [
            shape((rows, channels), F32),
            shape((rows, RANK), F32),
            shape((channels, 2 * rows), BF16),
            shape((rows, LANES), F32),
            shape((sessions, heads), F32),
            shape((targets, rows), F32),
            shape((1, channels), F32),
            shape(session_head_state.shape, BF16),
        ],
        in_specs=[pl.BlockSpec(memory_space=pltpu.HBM)] * 12,
        out_specs=[vmem()] * (n_msg + 8),
        scratch_shapes=[pltpu.SMEM(v.shape, v.dtype) for v in smalls[:2]]
        + [pltpu.VMEM(v.shape, v.dtype) for v in smalls[2:]]
        + [
            pltpu.SemaphoreType.DMA((chunks,)),
            pltpu.SemaphoreType.DMA((len(smalls),)),
            pltpu.SMEM((batch_count,), jnp.int32),
        ],
        compiler_params=pltpu.CompilerParams(vmem_limit_bytes=16 << 20),
        cost_estimate=pl.CostEstimate(
            flops=2 * 32 * session_head_state.size,
            bytes_accessed=2 * session_head_state.size,
            transcendentals=0,
        ),
        name="front",
    )(*[pltpu.with_memory_space_constraint(v, pltpu.HBM) for v in (session_head_state, *smalls)])
    msgs = out[:n_msg]
    gated, squares, drive, b_rows, keep, place, gain, held_state = out[n_msg:]

    def exchange(blocks):
        if split:
            return [blocks[0]] + [
                lax.ppermute(
                    blocks[k], "batch", [(i, i ^ k) for i in range(batch_count)]
                )
                for k in range(1, batch_count)
            ]
        block = blocks[0].reshape(batch_count, per_owner, -1)
        block = lax.all_to_all(block, "batch", split_axis=0, concat_axis=0, tiled=True)
        return [block.reshape(targets, -1)]

    arrived = exchange(msgs)

    pair = 2
    updated = pl.pallas_call(
        functools.partial(state_kernel, pair),
        out_shape=pltpu.VMEM(session_head_state.shape, BF16),
        in_specs=[vmem(), vmem(), smem(), vmem()],
        out_specs=vmem(),
        compiler_params=pltpu.CompilerParams(vmem_limit_bytes=4 << 20),
        cost_estimate=pl.CostEstimate(
            flops=8 * session_head_state.size,
            bytes_accessed=4 * session_head_state.size,
            transcendentals=0,
        ),
        name="state",
    )(drive, b_rows, keep, held_state)
    arrived = lax.optimization_barrier((arrived, updated))[0]

    partial, pick = pl.pallas_call(
        functools.partial(down_kernel, n_msg),
        out_shape=[shape((targets, 2 * RANK), F32), shape((targets, LANES), F32)],
        in_specs=[vmem()] * (n_msg + 2),
        out_specs=[vmem()] * 2,
        compiler_params=pltpu.CompilerParams(vmem_limit_bytes=4 << 20),
        name="down",
    )(*arrived, adapter_down_weight, squares)

    if tensor_count in (2, 4):
        parts = [partial] + [
            lax.ppermute(partial, "tensor", [(i, i ^ k) for i in range(tensor_count)])
            for k in range(1, tensor_count)
        ]
    else:
        parts = [lax.psum(partial, "tensor")]

    out = pl.pallas_call(
        functools.partial(up_kernel, len(parts), n_msg, sessions),
        out_shape=[shape((msg_rows, channels), F32)] * n_msg + [shape((rows, LANES), F32)],
        in_specs=[vmem()] * (len(parts) + 2),
        out_specs=[vmem()] * (n_msg + 1),
        compiler_params=pltpu.CompilerParams(vmem_limit_bytes=4 << 20),
        name="up",
    )(*parts, pick, adapter_up_weight)
    terms, inverse = out[:n_msg], out[n_msg]
    returned = exchange(terms)

    normed = pl.pallas_call(
        norm_kernel,
        out_shape=shape((DECODE_STEPS, sessions, channels), BF16),
        in_specs=[vmem()] * 3,
        out_specs=vmem(),
        compiler_params=pltpu.CompilerParams(vmem_limit_bytes=4 << 20),
        name="norm",
    )(gated, inverse, gain)

    delta = pl.pallas_call(
        functools.partial(final_kernel, n_msg),
        out_shape=shape((DECODE_STEPS, sessions, channels), F32),
        in_specs=[vmem()] * (n_msg + 2),
        out_specs=vmem(),
        compiler_params=pltpu.CompilerParams(vmem_limit_bytes=4 << 20),
        name="final",
    )(*returned, place, inverse)
    return (updated, normed, delta)


def solution(mesh):
    placed = (
        P(("groups", "batch"), "tensor", None, None),
        P(None, ("groups", "batch"), "tensor"),
        P(None, ("groups", "batch"), "tensor"),
        P(None, ("groups", "batch"), None, None),
        P(None, ("groups", "batch"), None, None),
        P(None, ("groups", "batch"), "tensor"),
        P("tensor"),
        P("tensor"),
        P("tensor"),
        P("tensor"),
        P(("groups", "batch"), None, "tensor"),
        P(("groups", "batch"), None, "tensor"),
        P(("groups", "batch")),
        P("groups"),
    )
    return jax.shard_map(
        per_device,
        mesh=mesh,
        in_specs=placed,
        out_specs=(
            P(("groups", "batch"), "tensor", None, None),
            P(None, ("groups", "batch"), "tensor"),
            P(None, ("groups", "batch"), "tensor"),
        ),
        check_vma=False,
    )
```

```python
import functools

import jax
import jax.numpy as jnp
from jax import lax
from jax.experimental import pallas as pl
from jax.experimental.pallas import tpu as pltpu
from jax.sharding import PartitionSpec as P

HEAD_COUNT = 64
HEAD_CHANNELS = 64
GROUPS = 4
DECODE_STEPS = 2
RANK = 64
LANES = 128
PAIR = 2

adapter_scale = 2.0
norm_eps = 1e-05

F32 = jnp.float32
BF16 = jnp.bfloat16
HIGHEST = lax.Precision.HIGHEST
NT = (((1,), (1,)), ((), ()))


def iota(shape, axis):
    return lax.broadcasted_iota(jnp.int32, shape, axis)


def thirds(v):
    high = v.astype(BF16)
    rest = v - high.astype(F32)
    middle = rest.astype(BF16)
    return [high, middle, (rest - middle.astype(F32)).astype(BF16)]


def front_kernel(dims, *refs):
    sessions, heads, batch_count, capacity, adapters_held, chunks, depth, split = dims
    n_msg = batch_count if split else 1
    inputs, refs = refs[:12], refs[12:]
    msgs, refs = refs[:n_msg], refs[n_msg:]
    gated_ref, square_ref, drive_ref, b_ref, keep_ref, place_ref, gain_ref = refs[:7]
    held = refs[7]
    local, (sems, small_sems, counts) = refs[8:19], refs[19:]
    state = inputs[0]
    channels = heads * HEAD_CHANNELS
    rows = DECODE_STEPS * sessions
    part = sessions // chunks

    loads = [
        pltpu.make_async_copy(source, target, small_sems.at[i])
        for i, (source, target) in enumerate(zip(inputs[1:], local))
    ]
    for load in loads:
        load.start()
    copies = []
    for i in range(chunks):
        window = pl.ds(i * part, part)
        copy = pltpu.make_async_copy(state.at[window], held.at[window], sems.at[i])
        copies.append(copy)
    for copy in copies[:depth]:
        copy.start()
    adapter, slot_of, x, z, b, c, raw, bias, rate, skip, gain_rows = local
    me = lax.axis_index("batch")
    group = lax.axis_index("tensor") * heads // (HEAD_COUNT // GROUPS)
    for load in loads:
        load.wait()
    def pick_group(ref):
        values = ref[...].astype(F32).reshape(rows, GROUPS, LANES)
        return jnp.sum(jnp.where(iota(values.shape, 1) == group, values, 0.0), axis=1)

    b_rows = pick_group(b)
    c_rows = pick_group(c)
    b_ref[...] = b_rows
    row_session = iota((rows, LANES), 0) % sessions
    c_blocks = jnp.concatenate(
        [jnp.where(row_session == s, c_rows, 0.0).astype(BF16) for s in range(sessions)], axis=1
    )
    def read(i):
        copies[i].wait()
        if i + depth < chunks:
            copies[i + depth].start()
        lanes = slice(i * part * LANES, (i + 1) * part * LANES)
        block = jnp.concatenate(
            [held[i * part + s].reshape(channels, LANES) for s in range(part)], axis=1
        )
        return lax.dot_general(c_blocks[:, lanes], block, NT, preferred_element_type=F32)

    reads = read(0) + read(1)
    b1, b2 = b_rows[:sessions], b_rows[sessions:]
    c1, c2 = c_rows[:sessions], c_rows[sessions:]
    bc11 = jnp.sum(b1 * c1, axis=1, keepdims=True)
    bc12 = jnp.sum(b1 * c2, axis=1, keepdims=True)
    bc22 = jnp.sum(b2 * c2, axis=1, keepdims=True)

    def softplus(v):
        return jnp.maximum(v, 0.0) + jnp.log1p(jnp.exp(-jnp.abs(v)))

    step1 = softplus(raw[0] + bias[...])
    step2 = softplus(raw[1] + bias[...])
    speed = -jnp.exp(rate[...])
    decay1 = jnp.exp(speed * step1)
    decay2 = jnp.exp(speed * step2)
    keep = decay1 * decay2
    keep_ref[...] = keep
    factors = jnp.concatenate(
        [
            decay1,
            step1 * bc11 + skip[...],
            keep,
            decay2 * step1 * bc12,
            step2 * bc22 + skip[...],
            decay2 * step1,
            step2,
        ],
        axis=0,
    )
    reads = reads + read(2) + read(3)
    gain = jnp.concatenate(
        [gain_rows[i : i + 1].astype(F32) for i in range(channels // LANES)], axis=1
    )
    gain_ref[...] = gain
    spread = (iota((heads, channels), 1) // HEAD_CHANNELS == iota((heads, channels), 0)).astype(F32)
    wide = jnp.dot(
        jnp.concatenate(thirds(factors), axis=1),
        jnp.concatenate([spread] * 3, axis=0).astype(BF16),
        preferred_element_type=F32,
    )
    wide = [wide[i * sessions : (i + 1) * sessions] for i in range(7)]
    x1 = x[0].astype(F32)
    x2 = x[1].astype(F32)
    drive = jnp.concatenate([wide[5] * x1, wide[6] * x2], axis=0)
    base1 = x1 * wide[1]
    base2 = x1 * wide[3] + x2 * wide[4]
    gates = jnp.concatenate([z[0].astype(F32), z[1].astype(F32)], axis=0)
    gates = gates / (1.0 + jnp.exp(-gates))
    base = jnp.concatenate([base1, base2], axis=0)
    scale = jnp.concatenate([wide[0], wide[2]], axis=0)
    reads = reads + read(4) + read(5)
    high = drive.astype(BF16)
    low = (drive - high.astype(F32)).astype(BF16)
    drive_ref[...] = jnp.concatenate([high, low], axis=0).T
    for i in range(batch_count):
        counts[i] = 0
    per_owner = DECODE_STEPS * capacity
    targets = batch_count * per_owner
    to = iota((targets, rows), 0)
    source = iota((targets, rows), 1)
    lane_to = iota((targets, LANES), 0)
    place = jnp.zeros((targets, rows), F32)
    pick = jnp.zeros((targets, LANES), F32)
    for s in range(sessions):
        slot = slot_of[adapter[s]]
        owner = slot // adapters_held
        which = (slot - owner * adapters_held).astype(F32)
        earlier = counts[owner]
        counts[owner] = earlier + 1
        relative = (owner ^ me) if split else owner
        first = relative * per_owner + earlier * DECODE_STEPS
        hit = (to - first == source // sessions) & (source % sessions == s)
        place = jnp.where(hit, 1.0, place)
        mine = (lane_to >= first) & (lane_to < first + DECODE_STEPS)
        pick = jnp.where(mine, which, pick)
    place_ref[...] = place
    place_bf = place.astype(BF16)

    reads = reads + read(6) + read(7)
    gated = (scale * reads + base) * gates
    gated_ref[...] = gated
    squares = jnp.zeros((rows, LANES), F32)
    for j in range(channels // LANES):
        piece = gated[:, j * LANES : (j + 1) * LANES]
        squares = squares + piece * piece
    weighted = (gated * gain).astype(BF16)
    packed = jnp.dot(place_bf, weighted, preferred_element_type=F32)
    for k in range(n_msg):
        n = targets // n_msg
        msgs[k][:, :channels] = packed[k * n : (k + 1) * n].astype(BF16)
    for k in range(n_msg):
        n = targets // n_msg
        msgs[k][:, channels:] = pick[k * n : (k + 1) * n].astype(BF16)
    square_ref[...] = squares[:, :RANK] + squares[:, RANK:]


def advance_state(first, count, left, b, keep, state, made):
    heads = state.shape[1]
    rows = b.shape[0]
    row_session = iota((rows, LANES), 0) % (rows // DECODE_STEPS)
    b_rows = b[...]
    kept_all = keep[...]
    for start in range(0, count, PAIR):
        right = jnp.concatenate(
            [
                jnp.where(row_session == first + start + q, b_rows, 0.0)
                for q in range(PAIR)
            ],
            axis=1,
        )
        right = jnp.concatenate([right, right], axis=0).astype(BF16)
        for h in range(heads):
            piece = slice(h * HEAD_CHANNELS, (h + 1) * HEAD_CHANNELS)
            added = jnp.dot(left[piece], right, preferred_element_type=F32)
            for q in range(PAIR):
                s = first + start + q
                kept = state[s, h].astype(F32) * kept_all[s : s + 1, h : h + 1]
                new = kept + added[:, q * LANES : (q + 1) * LANES]
                made[start + q, h] = new.astype(BF16)


def state_kernel(first, left, b, keep, state, made):
    advance_state(first, made.shape[0], left, b, keep, state, made)


def close_kernel(gated, inverse, gain, made, normed, out, rows, sems):
    store_state = pltpu.make_async_copy(made, out, sems.at[0])
    store_state.start()
    scaled = gated[...] * inverse[:, :1] * gain[...]
    rows[...] = scaled.astype(BF16).reshape(rows.shape)
    store_rows = pltpu.make_async_copy(rows, normed, sems.at[1])
    store_rows.start()
    store_state.wait()
    store_rows.wait()


def down_kernel(order, *refs):
    n_msg = len(order)
    msgs = [refs[order.index(k)] for k in range(n_msg)]
    down, squares, out, pick_ref = refs[n_msg:]
    held, rank, channels = down.shape
    rows = jnp.concatenate([m[...].astype(F32) for m in msgs], axis=0)
    pick = rows[:, channels:]
    weights = down[...].reshape(held * rank, channels)
    ranks = lax.dot_general(
        rows[:, :channels].astype(BF16), weights, NT, preferred_element_type=F32
    )
    chosen = jnp.zeros((rows.shape[0], rank), F32)
    for j in range(held):
        chosen = jnp.where(pick[:, :rank] == j, ranks[:, j * rank : (j + 1) * rank], chosen)
    pick_ref[...] = pick
    n_squares = squares.shape[0]
    if n_squares < chosen.shape[0]:
        filled = jnp.concatenate(
            [squares[...], jnp.zeros((chosen.shape[0] - n_squares, rank), F32)], axis=0
        )
    else:
        filled = squares[...]
    out[...] = jnp.concatenate([chosen, filled], axis=1)


def up_kernel(n_sum, n_msg, sessions, *refs):
    parts = refs[:n_sum]
    pick, up = refs[n_sum : n_sum + 2]
    outs = refs[n_sum + 2 : n_sum + 2 + n_msg]
    inverse = refs[n_sum + 2 + n_msg]
    held, rank, channels = up.shape
    total = parts[0][...]
    for p in parts[1:]:
        total = total + p[...]
    ranks = total[:, :rank]
    left = jnp.concatenate(
        [jnp.where(pick[:, :rank] == j, ranks, 0.0) for j in range(held)], axis=1
    ).astype(BF16)
    terms = adapter_scale * jnp.dot(
        left, up[...].reshape(held * rank, channels), preferred_element_type=F32
    )
    n = terms.shape[0] // n_msg
    for k in range(n_msg):
        outs[k][...] = terms[k * n : (k + 1) * n]
    rows = DECODE_STEPS * sessions
    sums = jnp.sum(total[:rows, rank:], axis=1, keepdims=True)
    factor = lax.rsqrt(sums / (HEAD_COUNT * HEAD_CHANNELS) + norm_eps)
    inverse[...] = jnp.broadcast_to(factor, inverse.shape)


def final_kernel(order, *refs):
    n_msg = len(order)
    msgs = [refs[order.index(k)] for k in range(n_msg)]
    place, inverse, out = refs[n_msg:]
    terms = jnp.concatenate([m[...] for m in msgs], axis=0)
    one_hot = place[...].astype(BF16)
    mine = lax.dot_general(
        jnp.concatenate([one_hot] * 3, axis=0),
        jnp.concatenate(thirds(terms), axis=0),
        (((0,), (0,)), ((), ())),
        preferred_element_type=F32,
    )
    out[...] = (mine * inverse[:, :1]).reshape(out.shape)


def vmem():
    return pl.BlockSpec(memory_space=pltpu.VMEM)


def smem():
    return pl.BlockSpec(memory_space=pltpu.SMEM)


def shape(dims, dtype):
    return jax.ShapeDtypeStruct(dims, dtype)


def per_device(
    session_head_state,
    convolved_activation,
    gate_activations,
    state_input_projection,
    state_output_projection,
    raw_step_sizes,
    step_size_bias,
    log_decay_rate,
    skip_coefficient,
    group_norm_gain,
    adapter_down_weight,
    adapter_up_weight,
    adapter_per_session,
    adapter_storage_slot,
):
    sessions, heads, _, state_size = session_head_state.shape
    channels = heads * HEAD_CHANNELS
    rows = DECODE_STEPS * sessions
    batch_count = lax.axis_size("batch")
    tensor_count = lax.axis_size("tensor")
    capacity = max(2, (sessions + batch_count - 1) // batch_count)
    adapters_held = adapter_down_weight.shape[0]
    split = batch_count in (2, 4)
    per_owner = DECODE_STEPS * capacity
    targets = batch_count * per_owner
    n_msg = batch_count if split else 1
    chunks = 8
    depth = 5
    msg_rows = targets // n_msg
    dims = (sessions, heads, batch_count, capacity, adapters_held, chunks, depth, split)
    smalls = (
        adapter_per_session,
        adapter_storage_slot,
        convolved_activation,
        gate_activations,
        state_input_projection,
        state_output_projection,
        raw_step_sizes,
        step_size_bias.reshape(1, heads),
        log_decay_rate.reshape(1, heads),
        skip_coefficient.reshape(1, heads),
        group_norm_gain.reshape(channels // LANES, LANES),
    )
    out = pl.pallas_call(
        functools.partial(front_kernel, dims),
        out_shape=[shape((msg_rows, channels + LANES), BF16)] * n_msg
        + [
            shape((rows, channels), F32),
            shape((rows, RANK), F32),
            shape((channels, 2 * rows), BF16),
            shape((rows, LANES), F32),
            shape((sessions, heads), F32),
            shape((targets, rows), F32),
            shape((1, channels), F32),
            shape(session_head_state.shape, BF16),
        ],
        in_specs=[pl.BlockSpec(memory_space=pltpu.HBM)] * 12,
        out_specs=[vmem()] * (n_msg + 8),
        scratch_shapes=[pltpu.SMEM(v.shape, v.dtype) for v in smalls[:2]]
        + [pltpu.VMEM(v.shape, v.dtype) for v in smalls[2:]]
        + [
            pltpu.SemaphoreType.DMA((chunks,)),
            pltpu.SemaphoreType.DMA((len(smalls),)),
            pltpu.SMEM((batch_count,), jnp.int32),
        ],
        compiler_params=pltpu.CompilerParams(vmem_limit_bytes=16 << 20),
        cost_estimate=pl.CostEstimate(
            flops=2 * 32 * session_head_state.size,
            bytes_accessed=2 * session_head_state.size,
            transcendentals=0,
        ),
        name="front",
    )(*[pltpu.with_memory_space_constraint(v, pltpu.HBM) for v in (session_head_state, *smalls)])
    msgs = out[:n_msg]
    gated, squares, left, b_rows, keep, place, gain, held_state = out[n_msg:]

    def exchange(blocks):
        if split:
            return [blocks[0]] + [
                lax.ppermute(
                    blocks[k], "batch", [(i, i ^ k) for i in range(batch_count)]
                )
                for k in range(1, batch_count)
            ]
        block = blocks[0].reshape(batch_count, per_owner, -1)
        block = lax.all_to_all(block, "batch", split_axis=0, concat_axis=0, tiled=True)
        return [block.reshape(targets, -1)]

    order = [0] + list(range(n_msg - 1, 0, -1))
    arrived = exchange(msgs)
    arrived = [arrived[k] for k in order]

    in_hbm = pl.BlockSpec(memory_space=pltpu.HBM)
    one_state = session_head_state.shape[1:]
    middle = sessions
    small = pltpu.CompilerParams(vmem_limit_bytes=4 << 20)

    def cost(count):
        elements = count * heads * HEAD_CHANNELS * state_size
        return pl.CostEstimate(flops=8 * elements, bytes_accessed=4 * elements, transcendentals=0)

    made = pl.pallas_call(
        functools.partial(state_kernel, 0),
        out_shape=pltpu.VMEM((middle,) + one_state, BF16),
        in_specs=[vmem()] * 4,
        out_specs=vmem(),
        compiler_params=small,
        cost_estimate=cost(middle),
        name="state",
    )(left, b_rows, keep, held_state)
    arrived, made = lax.optimization_barrier((arrived, made))

    partial, pick = pl.pallas_call(
        functools.partial(down_kernel, order),
        out_shape=[shape((targets, 2 * RANK), F32), shape((targets, LANES), F32)],
        in_specs=[vmem()] * (n_msg + 2),
        out_specs=[vmem()] * 2,
        compiler_params=pltpu.CompilerParams(vmem_limit_bytes=4 << 20),
        name="down",
    )(*arrived, adapter_down_weight, squares)

    if tensor_count in (2, 4):
        parts = [partial] + [
            lax.ppermute(partial, "tensor", [(i, i ^ k) for i in range(tensor_count)])
            for k in range(1, tensor_count)
        ]
    else:
        parts = [lax.psum(partial, "tensor")]

    out = pl.pallas_call(
        functools.partial(up_kernel, len(parts), n_msg, sessions),
        out_shape=[shape((msg_rows, channels), F32)] * n_msg + [shape((rows, LANES), F32)],
        in_specs=[vmem()] * (len(parts) + 2),
        out_specs=[vmem()] * (n_msg + 1),
        compiler_params=pltpu.CompilerParams(vmem_limit_bytes=4 << 20),
        name="up",
    )(*parts, pick, adapter_up_weight)
    terms, inverse = out[:n_msg], out[n_msg]
    returned = exchange(terms)
    returned = [returned[k] for k in order]

    normed, updated = pl.pallas_call(
        close_kernel,
        out_shape=[
            pltpu.HBM((DECODE_STEPS, sessions, channels), BF16),
            pltpu.HBM(session_head_state.shape, BF16),
        ],
        in_specs=[vmem()] * 4,
        out_specs=[in_hbm, in_hbm],
        scratch_shapes=[
            pltpu.VMEM((DECODE_STEPS, sessions, channels), BF16),
            pltpu.SemaphoreType.DMA((2,)),
        ],
        compiler_params=small,
        cost_estimate=cost(sessions),
        name="close",
    )(gated, inverse, gain, made)

    delta = pl.pallas_call(
        functools.partial(final_kernel, order),
        out_shape=shape((DECODE_STEPS, sessions, channels), F32),
        in_specs=[vmem()] * (n_msg + 2),
        out_specs=vmem(),
        compiler_params=pltpu.CompilerParams(vmem_limit_bytes=4 << 20),
        name="final",
    )(*returned, place, inverse)
    return (updated, normed, delta)


def solution(mesh):
    placed = (
        P(("groups", "batch"), "tensor", None, None),
        P(None, ("groups", "batch"), "tensor"),
        P(None, ("groups", "batch"), "tensor"),
        P(None, ("groups", "batch"), None, None),
        P(None, ("groups", "batch"), None, None),
        P(None, ("groups", "batch"), "tensor"),
        P("tensor"),
        P("tensor"),
        P("tensor"),
        P("tensor"),
        P(("groups", "batch"), None, "tensor"),
        P(("groups", "batch"), None, "tensor"),
        P(("groups", "batch")),
        P("groups"),
    )
    return jax.shard_map(
        per_device,
        mesh=mesh,
        in_specs=placed,
        out_specs=(
            P(("groups", "batch"), "tensor", None, None),
            P(None, ("groups", "batch"), "tensor"),
            P(None, ("groups", "batch"), "tensor"),
        ),
        check_vma=False,
    )
```

```python
import functools

import jax
import jax.numpy as jnp
from jax import lax
from jax.experimental import pallas as pl
from jax.experimental.pallas import tpu as pltpu
from jax.sharding import PartitionSpec as P

HEAD_COUNT = 64
HEAD_CHANNELS = 64
GROUPS = 4
DECODE_STEPS = 2
RANK = 64
LANES = 128
PAIR = 2

adapter_scale = 2.0
norm_eps = 1e-05

F32 = jnp.float32
BF16 = jnp.bfloat16
HIGHEST = lax.Precision.HIGHEST
NT = (((1,), (1,)), ((), ()))


def iota(shape, axis):
    return lax.broadcasted_iota(jnp.int32, shape, axis)


def thirds(v):
    high = v.astype(BF16)
    rest = v - high.astype(F32)
    middle = rest.astype(BF16)
    return [high, middle, (rest - middle.astype(F32)).astype(BF16)]


def front_kernel(dims, *refs):
    sessions, heads, batch_count, capacity, adapters_held, chunks, depth, split = dims
    n_msg = batch_count if split else 1
    inputs, refs = refs[:12], refs[12:]
    msgs, refs = refs[:n_msg], refs[n_msg:]
    gated_ref, square_ref, drive_ref, b_ref, keep_ref, place_ref, gain_ref = refs[:7]
    held = refs[7]
    local, (sems, small_sems, counts) = refs[8:19], refs[19:]
    state = inputs[0]
    channels = heads * HEAD_CHANNELS
    rows = DECODE_STEPS * sessions
    part = sessions // chunks

    loads = [
        pltpu.make_async_copy(source, target, small_sems.at[i])
        for i, (source, target) in enumerate(zip(inputs[1:], local))
    ]
    for load in loads:
        load.start()
    copies = []
    for i in range(chunks):
        window = pl.ds(i * part, part)
        copy = pltpu.make_async_copy(state.at[window], held.at[window], sems.at[i])
        copies.append(copy)
    for copy in copies[:depth]:
        copy.start()
    adapter, slot_of, x, z, b, c, raw, bias, rate, skip, gain_rows = local
    me = lax.axis_index("batch")
    group = lax.axis_index("tensor") * heads // (HEAD_COUNT // GROUPS)
    for load in loads:
        load.wait()
    def pick_group(ref):
        values = ref[...].astype(F32).reshape(rows, GROUPS, LANES)
        return jnp.sum(jnp.where(iota(values.shape, 1) == group, values, 0.0), axis=1)

    b_rows = pick_group(b)
    c_rows = pick_group(c)
    b_ref[...] = b_rows
    row_session = iota((rows, LANES), 0) % sessions
    c_blocks = jnp.concatenate(
        [jnp.where(row_session == s, c_rows, 0.0).astype(BF16) for s in range(sessions)], axis=1
    )
    def read(i):
        copies[i].wait()
        if i + depth < chunks:
            copies[i + depth].start()
        lanes = slice(i * part * LANES, (i + 1) * part * LANES)
        block = jnp.concatenate(
            [held[i * part + s].reshape(channels, LANES) for s in range(part)], axis=1
        )
        return lax.dot_general(c_blocks[:, lanes], block, NT, preferred_element_type=F32)

    reads = read(0) + read(1)
    b1, b2 = b_rows[:sessions], b_rows[sessions:]
    c1, c2 = c_rows[:sessions], c_rows[sessions:]
    bc11 = jnp.sum(b1 * c1, axis=1, keepdims=True)
    bc12 = jnp.sum(b1 * c2, axis=1, keepdims=True)
    bc22 = jnp.sum(b2 * c2, axis=1, keepdims=True)

    def softplus(v):
        return jnp.maximum(v, 0.0) + jnp.log1p(jnp.exp(-jnp.abs(v)))

    step1 = softplus(raw[0] + bias[...])
    step2 = softplus(raw[1] + bias[...])
    speed = -jnp.exp(rate[...])
    decay1 = jnp.exp(speed * step1)
    decay2 = jnp.exp(speed * step2)
    keep = decay1 * decay2
    keep_ref[...] = keep
    factors = jnp.concatenate(
        [
            decay1,
            step1 * bc11 + skip[...],
            keep,
            decay2 * step1 * bc12,
            step2 * bc22 + skip[...],
            decay2 * step1,
            step2,
        ],
        axis=0,
    )
    reads = reads + read(2) + read(3)
    gain = jnp.concatenate(
        [gain_rows[i : i + 1].astype(F32) for i in range(channels // LANES)], axis=1
    )
    gain_ref[...] = gain
    spread = (iota((heads, channels), 1) // HEAD_CHANNELS == iota((heads, channels), 0)).astype(F32)
    wide = jnp.dot(
        jnp.concatenate(thirds(factors), axis=1),
        jnp.concatenate([spread] * 3, axis=0).astype(BF16),
        preferred_element_type=F32,
    )
    wide = [wide[i * sessions : (i + 1) * sessions] for i in range(7)]
    x1 = x[0].astype(F32)
    x2 = x[1].astype(F32)
    drive = jnp.concatenate([wide[5] * x1, wide[6] * x2], axis=0)
    base1 = x1 * wide[1]
    base2 = x1 * wide[3] + x2 * wide[4]
    gates = jnp.concatenate([z[0].astype(F32), z[1].astype(F32)], axis=0)
    gates = gates / (1.0 + jnp.exp(-gates))
    base = jnp.concatenate([base1, base2], axis=0)
    scale = jnp.concatenate([wide[0], wide[2]], axis=0)
    reads = reads + read(4) + read(5)
    high = drive.astype(BF16)
    low = (drive - high.astype(F32)).astype(BF16)
    drive_ref[...] = jnp.concatenate([high, low], axis=0).T
    for i in range(batch_count):
        counts[i] = 0
    per_owner = DECODE_STEPS * capacity
    targets = batch_count * per_owner
    to = iota((targets, rows), 0)
    source = iota((targets, rows), 1)
    lane_to = iota((targets, LANES), 0)
    place = jnp.zeros((targets, rows), F32)
    pick = jnp.zeros((targets, LANES), F32)
    for s in range(sessions):
        slot = slot_of[adapter[s]]
        owner = slot // adapters_held
        which = (slot - owner * adapters_held).astype(F32)
        earlier = counts[owner]
        counts[owner] = earlier + 1
        relative = (owner ^ me) if split else owner
        first = relative * per_owner + earlier * DECODE_STEPS
        hit = (to - first == source // sessions) & (source % sessions == s)
        place = jnp.where(hit, 1.0, place)
        mine = (lane_to >= first) & (lane_to < first + DECODE_STEPS)
        pick = jnp.where(mine, which, pick)
    place_ref[...] = place.T.astype(BF16)
    place_bf = place.astype(BF16)

    reads = reads + read(6) + read(7)
    gated = (scale * reads + base) * gates
    gated_ref[...] = gated
    squares = jnp.zeros((rows, LANES), F32)
    for j in range(channels // LANES):
        piece = gated[:, j * LANES : (j + 1) * LANES]
        squares = squares + piece * piece
    weighted = (gated * gain).astype(BF16)
    packed = jnp.dot(place_bf, weighted, preferred_element_type=F32)
    for k in range(n_msg):
        n = targets // n_msg
        msgs[k][:, :channels] = packed[k * n : (k + 1) * n].astype(BF16)
    for k in range(n_msg):
        n = targets // n_msg
        msgs[k][:, channels:] = pick[k * n : (k + 1) * n].astype(BF16)
    square_ref[...] = squares[:, :RANK] + squares[:, RANK:]


def advance_state(first, count, left, b, keep, state, made):
    heads = state.shape[1]
    rows = b.shape[0]
    row_session = iota((rows, LANES), 0) % (rows // DECODE_STEPS)
    b_rows = b[...]
    kept_all = keep[...]
    for start in range(0, count, PAIR):
        right = jnp.concatenate(
            [
                jnp.where(row_session == first + start + q, b_rows, 0.0)
                for q in range(PAIR)
            ],
            axis=1,
        )
        right = jnp.concatenate([right, right], axis=0).astype(BF16)
        for h in range(heads):
            piece = slice(h * HEAD_CHANNELS, (h + 1) * HEAD_CHANNELS)
            added = jnp.dot(left[piece], right, preferred_element_type=F32)
            for q in range(PAIR):
                s = first + start + q
                kept = state[s, h].astype(F32) * kept_all[s : s + 1, h : h + 1]
                new = kept + added[:, q * LANES : (q + 1) * LANES]
                made[start + q, h] = new.astype(BF16)


def state_kernel(first, left, b, keep, state, made):
    advance_state(first, made.shape[0], left, b, keep, state, made)


def close_kernel(gated, inverse, gain, made, normed, out, rows, sems):
    store_state = pltpu.make_async_copy(made, out, sems.at[0])
    store_state.start()
    scaled = gated[...] * inverse[:, :1] * gain[...]
    rows[...] = scaled.astype(BF16).reshape(rows.shape)
    store_rows = pltpu.make_async_copy(rows, normed, sems.at[1])
    store_rows.start()
    store_state.wait()
    store_rows.wait()


def down_kernel(order, *refs):
    n_msg = len(order)
    msgs = [refs[order.index(k)] for k in range(n_msg)]
    down, squares, out, pick_ref = refs[n_msg:]
    held, rank, channels = down.shape
    rows = jnp.concatenate([m[...].astype(F32) for m in msgs], axis=0)
    pick = rows[:, channels:]
    weights = down[...].reshape(held * rank, channels)
    ranks = lax.dot_general(
        rows[:, :channels].astype(BF16), weights, NT, preferred_element_type=F32
    )
    chosen = jnp.zeros((rows.shape[0], rank), F32)
    for j in range(held):
        chosen = jnp.where(pick[:, :rank] == j, ranks[:, j * rank : (j + 1) * rank], chosen)
    pick_ref[...] = pick
    n_squares = squares.shape[0]
    if n_squares < chosen.shape[0]:
        filled = jnp.concatenate(
            [squares[...], jnp.zeros((chosen.shape[0] - n_squares, rank), F32)], axis=0
        )
    else:
        filled = squares[...]
    out[...] = jnp.concatenate([chosen, filled], axis=1)


def up_kernel(n_sum, n_msg, sessions, *refs):
    parts = refs[:n_sum]
    pick, up = refs[n_sum : n_sum + 2]
    outs = refs[n_sum + 2 : n_sum + 2 + n_msg]
    inverse = refs[n_sum + 2 + n_msg]
    held, rank, channels = up.shape
    total = parts[0][...]
    for p in parts[1:]:
        total = total + p[...]
    ranks = total[:, :rank]
    left = jnp.concatenate(
        [jnp.where(pick[:, :rank] == j, ranks, 0.0) for j in range(held)], axis=1
    ).astype(BF16)
    terms = adapter_scale * jnp.dot(
        left, up[...].reshape(held * rank, channels), preferred_element_type=F32
    )
    n = terms.shape[0] // n_msg
    for k in range(n_msg):
        outs[k][...] = terms[k * n : (k + 1) * n].astype(BF16)
    rows = DECODE_STEPS * sessions
    sums = jnp.sum(total[:rows, rank:], axis=1, keepdims=True)
    factor = lax.rsqrt(sums / (HEAD_COUNT * HEAD_CHANNELS) + norm_eps)
    inverse[...] = jnp.broadcast_to(factor, inverse.shape)


def final_kernel(order, *refs):
    n_msg = len(order)
    msgs = [refs[order.index(k)] for k in range(n_msg)]
    place, inverse, out = refs[n_msg:]
    terms = jnp.concatenate([m[...].astype(F32) for m in msgs], axis=0)
    mine = jnp.dot(place[...], terms.astype(BF16), preferred_element_type=F32)
    out[...] = (mine * inverse[:, :1]).reshape(out.shape)


def vmem():
    return pl.BlockSpec(memory_space=pltpu.VMEM)


def smem():
    return pl.BlockSpec(memory_space=pltpu.SMEM)


def shape(dims, dtype):
    return jax.ShapeDtypeStruct(dims, dtype)


def per_device(
    session_head_state,
    convolved_activation,
    gate_activations,
    state_input_projection,
    state_output_projection,
    raw_step_sizes,
    step_size_bias,
    log_decay_rate,
    skip_coefficient,
    group_norm_gain,
    adapter_down_weight,
    adapter_up_weight,
    adapter_per_session,
    adapter_storage_slot,
):
    sessions, heads, _, state_size = session_head_state.shape
    channels = heads * HEAD_CHANNELS
    rows = DECODE_STEPS * sessions
    batch_count = lax.axis_size("batch")
    tensor_count = lax.axis_size("tensor")
    capacity = max(2, (sessions + batch_count - 1) // batch_count)
    adapters_held = adapter_down_weight.shape[0]
    split = batch_count in (2, 4)
    per_owner = DECODE_STEPS * capacity
    targets = batch_count * per_owner
    n_msg = batch_count if split else 1
    chunks = 8
    depth = 5
    msg_rows = targets // n_msg
    dims = (sessions, heads, batch_count, capacity, adapters_held, chunks, depth, split)
    smalls = (
        adapter_per_session,
        adapter_storage_slot,
        convolved_activation,
        gate_activations,
        state_input_projection,
        state_output_projection,
        raw_step_sizes,
        step_size_bias.reshape(1, heads),
        log_decay_rate.reshape(1, heads),
        skip_coefficient.reshape(1, heads),
        group_norm_gain.reshape(channels // LANES, LANES),
    )
    out = pl.pallas_call(
        functools.partial(front_kernel, dims),
        out_shape=[shape((msg_rows, channels + LANES), BF16)] * n_msg
        + [
            shape((rows, channels), F32),
            shape((rows, RANK), F32),
            shape((channels, 2 * rows), BF16),
            shape((rows, LANES), F32),
            shape((sessions, heads), F32),
            shape((rows, targets), BF16),
            shape((1, channels), F32),
            shape(session_head_state.shape, BF16),
        ],
        in_specs=[pl.BlockSpec(memory_space=pltpu.HBM)] * 12,
        out_specs=[vmem()] * (n_msg + 8),
        scratch_shapes=[pltpu.SMEM(v.shape, v.dtype) for v in smalls[:2]]
        + [pltpu.VMEM(v.shape, v.dtype) for v in smalls[2:]]
        + [
            pltpu.SemaphoreType.DMA((chunks,)),
            pltpu.SemaphoreType.DMA((len(smalls),)),
            pltpu.SMEM((batch_count,), jnp.int32),
        ],
        compiler_params=pltpu.CompilerParams(vmem_limit_bytes=16 << 20),
        cost_estimate=pl.CostEstimate(
            flops=2 * 32 * session_head_state.size,
            bytes_accessed=2 * session_head_state.size,
            transcendentals=0,
        ),
        name="front",
    )(*[pltpu.with_memory_space_constraint(v, pltpu.HBM) for v in (session_head_state, *smalls)])
    msgs = out[:n_msg]
    gated, squares, left, b_rows, keep, place, gain, held_state = out[n_msg:]

    def exchange(blocks):
        if split:
            return [blocks[0]] + [
                lax.ppermute(
                    blocks[k], "batch", [(i, i ^ k) for i in range(batch_count)]
                )
                for k in range(1, batch_count)
            ]
        block = blocks[0].reshape(batch_count, per_owner, -1)
        block = lax.all_to_all(block, "batch", split_axis=0, concat_axis=0, tiled=True)
        return [block.reshape(targets, -1)]

    order = [0] + list(range(n_msg - 1, 0, -1))
    arrived = exchange(msgs)
    arrived = [arrived[k] for k in order]

    in_hbm = pl.BlockSpec(memory_space=pltpu.HBM)
    one_state = session_head_state.shape[1:]
    middle = sessions
    small = pltpu.CompilerParams(vmem_limit_bytes=4 << 20)

    def cost(count):
        elements = count * heads * HEAD_CHANNELS * state_size
        return pl.CostEstimate(flops=8 * elements, bytes_accessed=4 * elements, transcendentals=0)

    made = pl.pallas_call(
        functools.partial(state_kernel, 0),
        out_shape=pltpu.VMEM((middle,) + one_state, BF16),
        in_specs=[vmem()] * 4,
        out_specs=vmem(),
        compiler_params=small,
        cost_estimate=cost(middle),
        name="state",
    )(left, b_rows, keep, held_state)
    arrived, made = lax.optimization_barrier((arrived, made))

    partial, pick = pl.pallas_call(
        functools.partial(down_kernel, order),
        out_shape=[shape((targets, 2 * RANK), F32), shape((targets, LANES), F32)],
        in_specs=[vmem()] * (n_msg + 2),
        out_specs=[vmem()] * 2,
        compiler_params=pltpu.CompilerParams(vmem_limit_bytes=4 << 20),
        name="down",
    )(*arrived, adapter_down_weight, squares)

    if tensor_count in (2, 4):
        parts = [partial] + [
            lax.ppermute(partial, "tensor", [(i, i ^ k) for i in range(tensor_count)])
            for k in range(1, tensor_count)
        ]
    else:
        parts = [lax.psum(partial, "tensor")]

    out = pl.pallas_call(
        functools.partial(up_kernel, len(parts), n_msg, sessions),
        out_shape=[shape((msg_rows, channels), BF16)] * n_msg + [shape((rows, LANES), F32)],
        in_specs=[vmem()] * (len(parts) + 2),
        out_specs=[vmem()] * (n_msg + 1),
        compiler_params=pltpu.CompilerParams(vmem_limit_bytes=4 << 20),
        name="up",
    )(*parts, pick, adapter_up_weight)
    terms, inverse = out[:n_msg], out[n_msg]
    returned = exchange(terms)
    returned = [returned[k] for k in order]

    normed, updated = pl.pallas_call(
        close_kernel,
        out_shape=[
            pltpu.HBM((DECODE_STEPS, sessions, channels), BF16),
            pltpu.HBM(session_head_state.shape, BF16),
        ],
        in_specs=[vmem()] * 4,
        out_specs=[in_hbm, in_hbm],
        scratch_shapes=[
            pltpu.VMEM((DECODE_STEPS, sessions, channels), BF16),
            pltpu.SemaphoreType.DMA((2,)),
        ],
        compiler_params=small,
        cost_estimate=cost(sessions),
        name="close",
    )(gated, inverse, gain, made)

    delta = pl.pallas_call(
        functools.partial(final_kernel, order),
        out_shape=shape((DECODE_STEPS, sessions, channels), F32),
        in_specs=[vmem()] * (n_msg + 2),
        out_specs=vmem(),
        compiler_params=pltpu.CompilerParams(vmem_limit_bytes=4 << 20),
        name="final",
    )(*returned, place, inverse)
    return (updated, normed, delta)


def solution(mesh):
    placed = (
        P(("groups", "batch"), "tensor", None, None),
        P(None, ("groups", "batch"), "tensor"),
        P(None, ("groups", "batch"), "tensor"),
        P(None, ("groups", "batch"), None, None),
        P(None, ("groups", "batch"), None, None),
        P(None, ("groups", "batch"), "tensor"),
        P("tensor"),
        P("tensor"),
        P("tensor"),
        P("tensor"),
        P(("groups", "batch"), None, "tensor"),
        P(("groups", "batch"), None, "tensor"),
        P(("groups", "batch")),
        P("groups"),
    )
    return jax.shard_map(
        per_device,
        mesh=mesh,
        in_specs=placed,
        out_specs=(
            P(("groups", "batch"), "tensor", None, None),
            P(None, ("groups", "batch"), "tensor"),
            P(None, ("groups", "batch"), "tensor"),
        ),
        check_vma=False,
    )
```

```python
import functools

import jax
import jax.numpy as jnp
from jax import lax
from jax.experimental import pallas as pl
from jax.experimental.pallas import tpu as pltpu
from jax.sharding import PartitionSpec as P

HEAD_COUNT = 64
HEAD_CHANNELS = 64
GROUPS = 4
DECODE_STEPS = 2
RANK = 64
LANES = 128
PAIR = 2

adapter_scale = 2.0
norm_eps = 1e-05

F32 = jnp.float32
BF16 = jnp.bfloat16
HIGHEST = lax.Precision.HIGHEST
NT = (((1,), (1,)), ((), ()))


def iota(shape, axis):
    return lax.broadcasted_iota(jnp.int32, shape, axis)


def thirds(v):
    high = v.astype(BF16)
    rest = v - high.astype(F32)
    middle = rest.astype(BF16)
    return [high, middle, (rest - middle.astype(F32)).astype(BF16)]


def front_kernel(dims, *refs):
    sessions, heads, batch_count, capacity, adapters_held, chunks, depth, split = dims
    n_msg = batch_count if split else 1
    inputs, refs = refs[:12], refs[12:]
    msgs, refs = refs[:n_msg], refs[n_msg:]
    gated_ref, square_ref, drive_ref, b_ref, keep_ref, place_ref, gain_ref = refs[:7]
    held = refs[7]
    local, (sems, small_sems, counts) = refs[8:19], refs[19:]
    state = inputs[0]
    channels = heads * HEAD_CHANNELS
    rows = DECODE_STEPS * sessions
    part = sessions // chunks

    loads = [
        pltpu.make_async_copy(source, target, small_sems.at[i])
        for i, (source, target) in enumerate(zip(inputs[1:], local))
    ]
    first, later = loads[4:10], loads[:4] + loads[10:]
    for load in first:
        load.start()
    copies = []
    for i in range(chunks):
        window = pl.ds(i * part, part)
        copy = pltpu.make_async_copy(state.at[window], held.at[window], sems.at[i])
        copies.append(copy)
    for copy in copies[:depth]:
        copy.start()
    for load in later:
        load.start()
    adapter, slot_of, x, z, b, c, raw, bias, rate, skip, gain_rows = local
    me = lax.axis_index("batch")
    group = lax.axis_index("tensor") * heads // (HEAD_COUNT // GROUPS)
    for load in first[:2]:
        load.wait()
    def pick_group(ref):
        values = ref[...].astype(F32).reshape(rows, GROUPS, LANES)
        return jnp.sum(jnp.where(iota(values.shape, 1) == group, values, 0.0), axis=1)

    b_rows = pick_group(b)
    c_rows = pick_group(c)
    b_ref[...] = b_rows
    row_session = iota((rows, LANES), 0) % sessions
    c_blocks = jnp.concatenate(
        [jnp.where(row_session == s, c_rows, 0.0).astype(BF16) for s in range(sessions)], axis=1
    )
    def read(i):
        copies[i].wait()
        if i + depth < chunks:
            copies[i + depth].start()
        lanes = slice(i * part * LANES, (i + 1) * part * LANES)
        block = jnp.concatenate(
            [held[i * part + s].reshape(channels, LANES) for s in range(part)], axis=1
        )
        return lax.dot_general(c_blocks[:, lanes], block, NT, preferred_element_type=F32)

    reads = read(0) + read(1)
    for load in first[2:] + later:
        load.wait()
    b1, b2 = b_rows[:sessions], b_rows[sessions:]
    c1, c2 = c_rows[:sessions], c_rows[sessions:]
    bc11 = jnp.sum(b1 * c1, axis=1, keepdims=True)
    bc12 = jnp.sum(b1 * c2, axis=1, keepdims=True)
    bc22 = jnp.sum(b2 * c2, axis=1, keepdims=True)

    def softplus(v):
        return jnp.maximum(v, 0.0) + jnp.log1p(jnp.exp(-jnp.abs(v)))

    step1 = softplus(raw[0] + bias[...])
    step2 = softplus(raw[1] + bias[...])
    speed = -jnp.exp(rate[...])
    decay1 = jnp.exp(speed * step1)
    decay2 = jnp.exp(speed * step2)
    keep = decay1 * decay2
    keep_ref[...] = keep
    factors = jnp.concatenate(
        [
            decay1,
            step1 * bc11 + skip[...],
            keep,
            decay2 * step1 * bc12,
            step2 * bc22 + skip[...],
            decay2 * step1,
            step2,
        ],
        axis=0,
    )
    reads = reads + read(2) + read(3)
    gain = jnp.concatenate(
        [gain_rows[i : i + 1].astype(F32) for i in range(channels // LANES)], axis=1
    )
    gain_ref[...] = gain
    spread = (iota((heads, channels), 1) // HEAD_CHANNELS == iota((heads, channels), 0)).astype(F32)
    wide = jnp.dot(
        jnp.concatenate(thirds(factors), axis=1),
        jnp.concatenate([spread] * 3, axis=0).astype(BF16),
        preferred_element_type=F32,
    )
    wide = [wide[i * sessions : (i + 1) * sessions] for i in range(7)]
    x1 = x[0].astype(F32)
    x2 = x[1].astype(F32)
    drive = jnp.concatenate([wide[5] * x1, wide[6] * x2], axis=0)
    base1 = x1 * wide[1]
    base2 = x1 * wide[3] + x2 * wide[4]
    gates = jnp.concatenate([z[0].astype(F32), z[1].astype(F32)], axis=0)
    gates = gates / (1.0 + jnp.exp(-gates))
    base = jnp.concatenate([base1, base2], axis=0)
    scale = jnp.concatenate([wide[0], wide[2]], axis=0)
    reads = reads + read(4) + read(5)
    high = drive.astype(BF16)
    low = (drive - high.astype(F32)).astype(BF16)
    drive_ref[...] = jnp.concatenate([high, low], axis=0).T
    for i in range(batch_count):
        counts[i] = 0
    per_owner = DECODE_STEPS * capacity
    targets = batch_count * per_owner
    to = iota((targets, rows), 0)
    source = iota((targets, rows), 1)
    lane_to = iota((targets, LANES), 0)
    place = jnp.zeros((targets, rows), F32)
    pick = jnp.zeros((targets, LANES), F32)
    for s in range(sessions):
        slot = slot_of[adapter[s]]
        owner = slot // adapters_held
        which = (slot - owner * adapters_held).astype(F32)
        earlier = counts[owner]
        counts[owner] = earlier + 1
        relative = (owner ^ me) if split else owner
        first = relative * per_owner + earlier * DECODE_STEPS
        hit = (to - first == source // sessions) & (source % sessions == s)
        place = jnp.where(hit, 1.0, place)
        mine = (lane_to >= first) & (lane_to < first + DECODE_STEPS)
        pick = jnp.where(mine, which, pick)
    place_ref[...] = place.T.astype(BF16)
    place_bf = place.astype(BF16)

    reads = reads + read(6) + read(7)
    gated = (scale * reads + base) * gates
    gated_ref[...] = gated
    squares = jnp.zeros((rows, LANES), F32)
    for j in range(channels // LANES):
        piece = gated[:, j * LANES : (j + 1) * LANES]
        squares = squares + piece * piece
    weighted = (gated * gain).astype(BF16)
    packed = jnp.dot(place_bf, weighted, preferred_element_type=F32)
    for k in range(n_msg):
        n = targets // n_msg
        msgs[k][:, :channels] = packed[k * n : (k + 1) * n].astype(BF16)
    for k in range(n_msg):
        n = targets // n_msg
        msgs[k][:, channels:] = pick[k * n : (k + 1) * n].astype(BF16)
    square_ref[...] = squares[:, :RANK] + squares[:, RANK:]


def advance_state(first, count, left, b, keep, state, made):
    heads = state.shape[1]
    rows = b.shape[0]
    row_session = iota((rows, LANES), 0) % (rows // DECODE_STEPS)
    b_rows = b[...]
    kept_all = keep[...]
    for start in range(0, count, PAIR):
        right = jnp.concatenate(
            [
                jnp.where(row_session == first + start + q, b_rows, 0.0)
                for q in range(PAIR)
            ],
            axis=1,
        )
        right = jnp.concatenate([right, right], axis=0).astype(BF16)
        for h in range(heads):
            piece = slice(h * HEAD_CHANNELS, (h + 1) * HEAD_CHANNELS)
            added = jnp.dot(left[piece], right, preferred_element_type=F32)
            for q in range(PAIR):
                s = first + start + q
                kept = state[s, h].astype(F32) * kept_all[s : s + 1, h : h + 1]
                new = kept + added[:, q * LANES : (q + 1) * LANES]
                made[start + q, h] = new.astype(BF16)


def state_kernel(first, left, b, keep, state, made):
    advance_state(first, made.shape[0], left, b, keep, state, made)


def close_kernel(gated, inverse, gain, made, normed, out, rows, sems):
    store_state = pltpu.make_async_copy(made, out, sems.at[0])
    store_state.start()
    scaled = gated[...] * inverse[:, :1] * gain[...]
    rows[...] = scaled.astype(BF16).reshape(rows.shape)
    store_rows = pltpu.make_async_copy(rows, normed, sems.at[1])
    store_rows.start()
    store_state.wait()
    store_rows.wait()


def down_kernel(order, *refs):
    n_msg = len(order)
    msgs = [refs[order.index(k)] for k in range(n_msg)]
    down, squares, out, pick_ref = refs[n_msg:]
    held, rank, channels = down.shape
    rows = jnp.concatenate([m[...].astype(F32) for m in msgs], axis=0)
    pick = rows[:, channels:]
    weights = down[...].reshape(held * rank, channels)
    ranks = lax.dot_general(
        rows[:, :channels].astype(BF16), weights, NT, preferred_element_type=F32
    )
    chosen = jnp.zeros((rows.shape[0], rank), F32)
    for j in range(held):
        chosen = jnp.where(pick[:, :rank] == j, ranks[:, j * rank : (j + 1) * rank], chosen)
    pick_ref[...] = pick
    n_squares = squares.shape[0]
    if n_squares < chosen.shape[0]:
        filled = jnp.concatenate(
            [squares[...], jnp.zeros((chosen.shape[0] - n_squares, rank), F32)], axis=0
        )
    else:
        filled = squares[...]
    out[...] = jnp.concatenate([chosen, filled], axis=1)


def up_kernel(n_sum, n_msg, sessions, *refs):
    parts = refs[:n_sum]
    pick, up = refs[n_sum : n_sum + 2]
    outs = refs[n_sum + 2 : n_sum + 2 + n_msg]
    inverse = refs[n_sum + 2 + n_msg]
    held, rank, channels = up.shape
    total = parts[0][...]
    for p in parts[1:]:
        total = total + p[...]
    ranks = total[:, :rank]
    left = jnp.concatenate(
        [jnp.where(pick[:, :rank] == j, ranks, 0.0) for j in range(held)], axis=1
    )
    high = left.astype(BF16)
    weights = up[...].reshape(held * rank, channels)
    both = jnp.dot(
        jnp.concatenate([left, left - high.astype(F32)], axis=0).astype(BF16),
        weights,
        preferred_element_type=F32,
    )
    terms = adapter_scale * (both[: left.shape[0]] + both[left.shape[0] :])
    n = terms.shape[0] // n_msg
    for k in range(n_msg):
        outs[k][...] = terms[k * n : (k + 1) * n].astype(BF16)
    rows = DECODE_STEPS * sessions
    sums = jnp.sum(total[:rows, rank:], axis=1, keepdims=True)
    factor = lax.rsqrt(sums / (HEAD_COUNT * HEAD_CHANNELS) + norm_eps)
    inverse[...] = jnp.broadcast_to(factor, inverse.shape)


def final_kernel(order, *refs):
    n_msg = len(order)
    msgs = [refs[order.index(k)] for k in range(n_msg)]
    place, inverse, out = refs[n_msg:]
    terms = jnp.concatenate([m[...].astype(F32) for m in msgs], axis=0)
    mine = jnp.dot(place[...], terms.astype(BF16), preferred_element_type=F32)
    out[...] = (mine * inverse[:, :1]).reshape(out.shape)


def vmem():
    return pl.BlockSpec(memory_space=pltpu.VMEM)


def smem():
    return pl.BlockSpec(memory_space=pltpu.SMEM)


def shape(dims, dtype):
    return jax.ShapeDtypeStruct(dims, dtype)


def per_device(
    session_head_state,
    convolved_activation,
    gate_activations,
    state_input_projection,
    state_output_projection,
    raw_step_sizes,
    step_size_bias,
    log_decay_rate,
    skip_coefficient,
    group_norm_gain,
    adapter_down_weight,
    adapter_up_weight,
    adapter_per_session,
    adapter_storage_slot,
):
    sessions, heads, _, state_size = session_head_state.shape
    channels = heads * HEAD_CHANNELS
    rows = DECODE_STEPS * sessions
    batch_count = lax.axis_size("batch")
    tensor_count = lax.axis_size("tensor")
    capacity = max(2, (sessions + batch_count - 1) // batch_count)
    adapters_held = adapter_down_weight.shape[0]
    split = batch_count in (2, 4)
    per_owner = DECODE_STEPS * capacity
    targets = batch_count * per_owner
    n_msg = batch_count if split else 1
    chunks = 8
    depth = 5
    msg_rows = targets // n_msg
    dims = (sessions, heads, batch_count, capacity, adapters_held, chunks, depth, split)
    smalls = (
        adapter_per_session,
        adapter_storage_slot,
        convolved_activation,
        gate_activations,
        state_input_projection,
        state_output_projection,
        raw_step_sizes,
        step_size_bias.reshape(1, heads),
        log_decay_rate.reshape(1, heads),
        skip_coefficient.reshape(1, heads),
        group_norm_gain.reshape(channels // LANES, LANES),
    )
    out = pl.pallas_call(
        functools.partial(front_kernel, dims),
        out_shape=[shape((msg_rows, channels + LANES), BF16)] * n_msg
        + [
            shape((rows, channels), F32),
            shape((rows, RANK), F32),
            shape((channels, 2 * rows), BF16),
            shape((rows, LANES), F32),
            shape((sessions, heads), F32),
            shape((rows, targets), BF16),
            shape((1, channels), F32),
            shape(session_head_state.shape, BF16),
        ],
        in_specs=[pl.BlockSpec(memory_space=pltpu.HBM)] * 12,
        out_specs=[vmem()] * (n_msg + 8),
        scratch_shapes=[pltpu.SMEM(v.shape, v.dtype) for v in smalls[:2]]
        + [pltpu.VMEM(v.shape, v.dtype) for v in smalls[2:]]
        + [
            pltpu.SemaphoreType.DMA((chunks,)),
            pltpu.SemaphoreType.DMA((len(smalls),)),
            pltpu.SMEM((batch_count,), jnp.int32),
        ],
        compiler_params=pltpu.CompilerParams(vmem_limit_bytes=16 << 20),
        cost_estimate=pl.CostEstimate(
            flops=2 * 32 * session_head_state.size,
            bytes_accessed=2 * session_head_state.size,
            transcendentals=0,
        ),
        name="front",
    )(*[pltpu.with_memory_space_constraint(v, pltpu.HBM) for v in (session_head_state, *smalls)])
    msgs = out[:n_msg]
    gated, squares, left, b_rows, keep, place, gain, held_state = out[n_msg:]

    def exchange(blocks):
        if split:
            return [blocks[0]] + [
                lax.ppermute(
                    blocks[k], "batch", [(i, i ^ k) for i in range(batch_count)]
                )
                for k in range(1, batch_count)
            ]
        block = blocks[0].reshape(batch_count, per_owner, -1)
        block = lax.all_to_all(block, "batch", split_axis=0, concat_axis=0, tiled=True)
        return [block.reshape(targets, -1)]

    order = [0] + list(range(n_msg - 1, 0, -1))
    arrived = exchange(msgs)
    arrived = [arrived[k] for k in order]

    in_hbm = pl.BlockSpec(memory_space=pltpu.HBM)
    one_state = session_head_state.shape[1:]
    middle = sessions
    small = pltpu.CompilerParams(vmem_limit_bytes=4 << 20)

    def cost(count):
        elements = count * heads * HEAD_CHANNELS * state_size
        return pl.CostEstimate(flops=8 * elements, bytes_accessed=4 * elements, transcendentals=0)

    made = pl.pallas_call(
        functools.partial(state_kernel, 0),
        out_shape=pltpu.VMEM((middle,) + one_state, BF16),
        in_specs=[vmem()] * 4,
        out_specs=vmem(),
        compiler_params=small,
        cost_estimate=cost(middle),
        name="state",
    )(left, b_rows, keep, held_state)
    arrived, made = lax.optimization_barrier((arrived, made))

    partial, pick = pl.pallas_call(
        functools.partial(down_kernel, order),
        out_shape=[shape((targets, 2 * RANK), F32), shape((targets, LANES), F32)],
        in_specs=[vmem()] * (n_msg + 2),
        out_specs=[vmem()] * 2,
        compiler_params=pltpu.CompilerParams(vmem_limit_bytes=4 << 20),
        name="down",
    )(*arrived, adapter_down_weight, squares)

    if tensor_count in (2, 4):
        parts = [partial] + [
            lax.ppermute(partial, "tensor", [(i, i ^ k) for i in range(tensor_count)])
            for k in range(1, tensor_count)
        ]
    else:
        parts = [lax.psum(partial, "tensor")]

    out = pl.pallas_call(
        functools.partial(up_kernel, len(parts), n_msg, sessions),
        out_shape=[shape((msg_rows, channels), BF16)] * n_msg + [shape((rows, LANES), F32)],
        in_specs=[vmem()] * (len(parts) + 2),
        out_specs=[vmem()] * (n_msg + 1),
        compiler_params=pltpu.CompilerParams(vmem_limit_bytes=4 << 20),
        name="up",
    )(*parts, pick, adapter_up_weight)
    terms, inverse = out[:n_msg], out[n_msg]
    returned = exchange(terms)
    returned = [returned[k] for k in order]

    normed, updated = pl.pallas_call(
        close_kernel,
        out_shape=[
            pltpu.HBM((DECODE_STEPS, sessions, channels), BF16),
            pltpu.HBM(session_head_state.shape, BF16),
        ],
        in_specs=[vmem()] * 4,
        out_specs=[in_hbm, in_hbm],
        scratch_shapes=[
            pltpu.VMEM((DECODE_STEPS, sessions, channels), BF16),
            pltpu.SemaphoreType.DMA((2,)),
        ],
        compiler_params=small,
        cost_estimate=cost(sessions),
        name="close",
    )(gated, inverse, gain, made)

    delta = pl.pallas_call(
        functools.partial(final_kernel, order),
        out_shape=shape((DECODE_STEPS, sessions, channels), F32),
        in_specs=[vmem()] * (n_msg + 2),
        out_specs=vmem(),
        compiler_params=pltpu.CompilerParams(vmem_limit_bytes=4 << 20),
        name="final",
    )(*returned, place, inverse)
    return (updated, normed, delta)


def solution(mesh):
    placed = (
        P(("groups", "batch"), "tensor", None, None),
        P(None, ("groups", "batch"), "tensor"),
        P(None, ("groups", "batch"), "tensor"),
        P(None, ("groups", "batch"), None, None),
        P(None, ("groups", "batch"), None, None),
        P(None, ("groups", "batch"), "tensor"),
        P("tensor"),
        P("tensor"),
        P("tensor"),
        P("tensor"),
        P(("groups", "batch"), None, "tensor"),
        P(("groups", "batch"), None, "tensor"),
        P(("groups", "batch")),
        P("groups"),
    )
    return jax.shard_map(
        per_device,
        mesh=mesh,
        in_specs=placed,
        out_specs=(
            P(("groups", "batch"), "tensor", None, None),
            P(None, ("groups", "batch"), "tensor"),
            P(None, ("groups", "batch"), "tensor"),
        ),
        check_vma=False,
    )
```

```python
import functools

import jax
import jax.numpy as jnp
from jax import lax
from jax.experimental import pallas as pl
from jax.experimental.pallas import tpu as pltpu
from jax.sharding import PartitionSpec as P

HEAD_COUNT = 64
HEAD_CHANNELS = 64
GROUPS = 4
DECODE_STEPS = 2
RANK = 64
LANES = 128
PAIR = 2

adapter_scale = 2.0
norm_eps = 1e-05

F32 = jnp.float32
BF16 = jnp.bfloat16
HIGHEST = lax.Precision.HIGHEST
NT = (((1,), (1,)), ((), ()))


def iota(shape, axis):
    return lax.broadcasted_iota(jnp.int32, shape, axis)


def thirds(v):
    high = v.astype(BF16)
    rest = v - high.astype(F32)
    middle = rest.astype(BF16)
    return [high, middle, (rest - middle.astype(F32)).astype(BF16)]


def front_kernel(dims, *refs):
    sessions, heads, batch_count, capacity, adapters_held, chunks, depth, split = dims
    n_msg = batch_count if split else 1
    inputs, refs = refs[:12], refs[12:]
    msgs, refs = refs[:n_msg], refs[n_msg:]
    gated_ref, square_ref, drive_ref, b_ref, keep_ref, place_ref, gain_ref = refs[:7]
    held = refs[7]
    local, (sems, small_sems, counts) = refs[8:19], refs[19:]
    state = inputs[0]
    channels = heads * HEAD_CHANNELS
    rows = DECODE_STEPS * sessions
    part = sessions // chunks

    loads = [
        pltpu.make_async_copy(source, target, small_sems.at[i])
        for i, (source, target) in enumerate(zip(inputs[1:], local))
    ]
    first, later = loads[4:10], loads[:4] + loads[10:]
    for load in first:
        load.start()
    copies = []
    for i in range(chunks):
        window = pl.ds(i * part, part)
        copy = pltpu.make_async_copy(state.at[window], held.at[window], sems.at[i])
        copies.append(copy)
    for copy in copies[:depth]:
        copy.start()
    for load in later:
        load.start()
    adapter, slot_of, x, z, b, c, raw, bias, rate, skip, gain_rows = local
    me = lax.axis_index("batch")
    group = lax.axis_index("tensor") * heads // (HEAD_COUNT // GROUPS)
    for load in first[:2]:
        load.wait()
    def pick_group(ref):
        values = ref[...].astype(F32).reshape(rows, GROUPS, LANES)
        return jnp.sum(jnp.where(iota(values.shape, 1) == group, values, 0.0), axis=1)

    b_rows = pick_group(b)
    c_rows = pick_group(c)
    b_ref[...] = b_rows
    row_session = iota((rows, LANES), 0) % sessions
    c_blocks = jnp.concatenate(
        [jnp.where(row_session == s, c_rows, 0.0).astype(BF16) for s in range(sessions)], axis=1
    )
    def read(i):
        copies[i].wait()
        if i + depth < chunks:
            copies[i + depth].start()
        lanes = slice(i * part * LANES, (i + 1) * part * LANES)
        block = jnp.concatenate(
            [held[i * part + s].reshape(channels, LANES) for s in range(part)], axis=1
        )
        quarter = channels // 4
        return jnp.concatenate(
            [
                lax.dot_general(
                    c_blocks[:, lanes],
                    block[q * quarter : (q + 1) * quarter],
                    NT,
                    preferred_element_type=F32,
                )
                for q in range(4)
            ],
            axis=1,
        )

    reads = read(0) + read(1)
    for load in first[2:] + later:
        load.wait()
    b1, b2 = b_rows[:sessions], b_rows[sessions:]
    c1, c2 = c_rows[:sessions], c_rows[sessions:]
    bc11 = jnp.sum(b1 * c1, axis=1, keepdims=True)
    bc12 = jnp.sum(b1 * c2, axis=1, keepdims=True)
    bc22 = jnp.sum(b2 * c2, axis=1, keepdims=True)

    def softplus(v):
        return jnp.maximum(v, 0.0) + jnp.log1p(jnp.exp(-jnp.abs(v)))

    step1 = softplus(raw[0] + bias[...])
    step2 = softplus(raw[1] + bias[...])
    speed = -jnp.exp(rate[...])
    decay1 = jnp.exp(speed * step1)
    decay2 = jnp.exp(speed * step2)
    keep = decay1 * decay2
    keep_ref[...] = keep
    factors = jnp.concatenate(
        [
            decay1,
            step1 * bc11 + skip[...],
            keep,
            decay2 * step1 * bc12,
            step2 * bc22 + skip[...],
            decay2 * step1,
            step2,
        ],
        axis=0,
    )
    reads = reads + read(2) + read(3)
    gain = jnp.concatenate(
        [gain_rows[i : i + 1].astype(F32) for i in range(channels // LANES)], axis=1
    )
    gain_ref[...] = gain
    spread = (iota((heads, channels), 1) // HEAD_CHANNELS == iota((heads, channels), 0)).astype(F32)
    wide = jnp.dot(
        jnp.concatenate(thirds(factors), axis=1),
        jnp.concatenate([spread] * 3, axis=0).astype(BF16),
        preferred_element_type=F32,
    )
    wide = [wide[i * sessions : (i + 1) * sessions] for i in range(7)]
    x1 = x[0].astype(F32)
    x2 = x[1].astype(F32)
    drive = jnp.concatenate([wide[5] * x1, wide[6] * x2], axis=0)
    base1 = x1 * wide[1]
    base2 = x1 * wide[3] + x2 * wide[4]
    gates = jnp.concatenate([z[0].astype(F32), z[1].astype(F32)], axis=0)
    gates = gates / (1.0 + jnp.exp(-gates))
    base = jnp.concatenate([base1, base2], axis=0)
    scale = jnp.concatenate([wide[0], wide[2]], axis=0)
    reads = reads + read(4) + read(5)
    high = drive.astype(BF16)
    low = (drive - high.astype(F32)).astype(BF16)
    drive_ref[...] = jnp.concatenate([high, low], axis=0).T
    for i in range(batch_count):
        counts[i] = 0
    per_owner = DECODE_STEPS * capacity
    targets = batch_count * per_owner
    to = iota((targets, rows), 0)
    source = iota((targets, rows), 1)
    lane_to = iota((targets, LANES), 0)
    place = jnp.zeros((targets, rows), F32)
    pick = jnp.zeros((targets, LANES), F32)
    for s in range(sessions):
        slot = slot_of[adapter[s]]
        owner = slot // adapters_held
        which = (slot - owner * adapters_held).astype(F32)
        earlier = counts[owner]
        counts[owner] = earlier + 1
        relative = (owner ^ me) if split else owner
        first = relative * per_owner + earlier * DECODE_STEPS
        hit = (to - first == source // sessions) & (source % sessions == s)
        place = jnp.where(hit, 1.0, place)
        mine = (lane_to >= first) & (lane_to < first + DECODE_STEPS)
        pick = jnp.where(mine, which, pick)
    place_ref[...] = place.T.astype(BF16)
    place_bf = place.astype(BF16)

    reads = reads + read(6) + read(7)
    gated = (scale * reads + base) * gates
    gated_ref[...] = gated
    squares = jnp.zeros((rows, LANES), F32)
    for j in range(channels // LANES):
        piece = gated[:, j * LANES : (j + 1) * LANES]
        squares = squares + piece * piece
    weighted = (gated * gain).astype(BF16)
    packed = jnp.dot(place_bf, weighted, preferred_element_type=F32)
    for k in range(n_msg):
        n = targets // n_msg
        msgs[k][:, :channels] = packed[k * n : (k + 1) * n].astype(BF16)
    for k in range(n_msg):
        n = targets // n_msg
        msgs[k][:, channels:] = pick[k * n : (k + 1) * n].astype(BF16)
    square_ref[...] = squares[:, :RANK] + squares[:, RANK:]


def advance_state(first, count, left, b, keep, state, made):
    heads = state.shape[1]
    rows = b.shape[0]
    row_session = iota((rows, LANES), 0) % (rows // DECODE_STEPS)
    b_rows = b[...]
    kept_all = keep[...]
    for start in range(0, count, PAIR):
        right = jnp.concatenate(
            [
                jnp.where(row_session == first + start + q, b_rows, 0.0)
                for q in range(PAIR)
            ],
            axis=1,
        )
        right = jnp.concatenate([right, right], axis=0).astype(BF16)
        for h in range(heads):
            piece = slice(h * HEAD_CHANNELS, (h + 1) * HEAD_CHANNELS)
            added = jnp.dot(left[piece], right, preferred_element_type=F32)
            for q in range(PAIR):
                s = first + start + q
                kept = state[s, h].astype(F32) * kept_all[s : s + 1, h : h + 1]
                new = kept + added[:, q * LANES : (q + 1) * LANES]
                made[start + q, h] = new.astype(BF16)


def state_kernel(first, left, b, keep, state, made):
    advance_state(first, made.shape[0], left, b, keep, state, made)


def close_kernel(gated, inverse, gain, made, normed, out, rows, sems):
    store_state = pltpu.make_async_copy(made, out, sems.at[0])
    store_state.start()
    scaled = gated[...] * inverse[:, :1] * gain[...]
    rows[...] = scaled.astype(BF16).reshape(rows.shape)
    store_rows = pltpu.make_async_copy(rows, normed, sems.at[1])
    store_rows.start()
    store_state.wait()
    store_rows.wait()


def down_kernel(order, *refs):
    n_msg = len(order)
    msgs = [refs[order.index(k)] for k in range(n_msg)]
    down, squares, out, pick_ref = refs[n_msg:]
    held, rank, channels = down.shape
    rows = jnp.concatenate([m[...].astype(F32) for m in msgs], axis=0)
    pick = rows[:, channels:]
    weights = down[...].reshape(held * rank, channels)
    ranks = lax.dot_general(
        rows[:, :channels].astype(BF16), weights, NT, preferred_element_type=F32
    )
    chosen = jnp.zeros((rows.shape[0], rank), F32)
    for j in range(held):
        chosen = jnp.where(pick[:, :rank] == j, ranks[:, j * rank : (j + 1) * rank], chosen)
    pick_ref[...] = pick
    n_squares = squares.shape[0]
    if n_squares < chosen.shape[0]:
        filled = jnp.concatenate(
            [squares[...], jnp.zeros((chosen.shape[0] - n_squares, rank), F32)], axis=0
        )
    else:
        filled = squares[...]
    out[...] = jnp.concatenate([chosen, filled], axis=1)


def up_kernel(n_sum, n_msg, sessions, *refs):
    parts = refs[:n_sum]
    pick, up = refs[n_sum : n_sum + 2]
    outs = refs[n_sum + 2 : n_sum + 2 + n_msg]
    inverse = refs[n_sum + 2 + n_msg]
    held, rank, channels = up.shape
    total = parts[0][...]
    for p in parts[1:]:
        total = total + p[...]
    ranks = total[:, :rank]
    left = jnp.concatenate(
        [jnp.where(pick[:, :rank] == j, ranks, 0.0) for j in range(held)], axis=1
    )
    high = left.astype(BF16)
    weights = up[...].reshape(held * rank, channels)
    both = jnp.dot(
        jnp.concatenate([left, left - high.astype(F32)], axis=0).astype(BF16),
        weights,
        preferred_element_type=F32,
    )
    terms = adapter_scale * (both[: left.shape[0]] + both[left.shape[0] :])
    n = terms.shape[0] // n_msg
    for k in range(n_msg):
        outs[k][...] = terms[k * n : (k + 1) * n].astype(BF16)
    rows = DECODE_STEPS * sessions
    sums = jnp.sum(total[:rows, rank:], axis=1, keepdims=True)
    factor = lax.rsqrt(sums / (HEAD_COUNT * HEAD_CHANNELS) + norm_eps)
    inverse[...] = jnp.broadcast_to(factor, inverse.shape)


def final_kernel(order, *refs):
    n_msg = len(order)
    msgs = [refs[order.index(k)] for k in range(n_msg)]
    place, inverse, out = refs[n_msg:]
    terms = jnp.concatenate([m[...].astype(F32) for m in msgs], axis=0)
    mine = jnp.dot(place[...], terms.astype(BF16), preferred_element_type=F32)
    out[...] = (mine * inverse[:, :1]).reshape(out.shape)


def vmem():
    return pl.BlockSpec(memory_space=pltpu.VMEM)


def smem():
    return pl.BlockSpec(memory_space=pltpu.SMEM)


def shape(dims, dtype):
    return jax.ShapeDtypeStruct(dims, dtype)


def per_device(
    session_head_state,
    convolved_activation,
    gate_activations,
    state_input_projection,
    state_output_projection,
    raw_step_sizes,
    step_size_bias,
    log_decay_rate,
    skip_coefficient,
    group_norm_gain,
    adapter_down_weight,
    adapter_up_weight,
    adapter_per_session,
    adapter_storage_slot,
):
    sessions, heads, _, state_size = session_head_state.shape
    channels = heads * HEAD_CHANNELS
    rows = DECODE_STEPS * sessions
    batch_count = lax.axis_size("batch")
    tensor_count = lax.axis_size("tensor")
    capacity = max(2, (sessions + batch_count - 1) // batch_count)
    adapters_held = adapter_down_weight.shape[0]
    split = batch_count in (2, 4)
    per_owner = DECODE_STEPS * capacity
    targets = batch_count * per_owner
    n_msg = batch_count if split else 1
    chunks = 8
    depth = 5
    msg_rows = targets // n_msg
    dims = (sessions, heads, batch_count, capacity, adapters_held, chunks, depth, split)
    smalls = (
        adapter_per_session,
        adapter_storage_slot,
        convolved_activation,
        gate_activations,
        state_input_projection,
        state_output_projection,
        raw_step_sizes,
        step_size_bias.reshape(1, heads),
        log_decay_rate.reshape(1, heads),
        skip_coefficient.reshape(1, heads),
        group_norm_gain.reshape(channels // LANES, LANES),
    )
    out = pl.pallas_call(
        functools.partial(front_kernel, dims),
        out_shape=[shape((msg_rows, channels + LANES), BF16)] * n_msg
        + [
            shape((rows, channels), F32),
            shape((rows, RANK), F32),
            shape((channels, 2 * rows), BF16),
            shape((rows, LANES), F32),
            shape((sessions, heads), F32),
            shape((rows, targets), BF16),
            shape((1, channels), F32),
            shape(session_head_state.shape, BF16),
        ],
        in_specs=[pl.BlockSpec(memory_space=pltpu.HBM)] * 12,
        out_specs=[vmem()] * (n_msg + 8),
        scratch_shapes=[pltpu.SMEM(v.shape, v.dtype) for v in smalls[:2]]
        + [pltpu.VMEM(v.shape, v.dtype) for v in smalls[2:]]
        + [
            pltpu.SemaphoreType.DMA((chunks,)),
            pltpu.SemaphoreType.DMA((len(smalls),)),
            pltpu.SMEM((batch_count,), jnp.int32),
        ],
        compiler_params=pltpu.CompilerParams(vmem_limit_bytes=16 << 20),
        cost_estimate=pl.CostEstimate(
            flops=2 * 32 * session_head_state.size,
            bytes_accessed=2 * session_head_state.size,
            transcendentals=0,
        ),
        name="front",
    )(*[pltpu.with_memory_space_constraint(v, pltpu.HBM) for v in (session_head_state, *smalls)])
    msgs = out[:n_msg]
    gated, squares, left, b_rows, keep, place, gain, held_state = out[n_msg:]

    def exchange(blocks):
        if split:
            return [blocks[0]] + [
                lax.ppermute(
                    blocks[k], "batch", [(i, i ^ k) for i in range(batch_count)]
                )
                for k in range(1, batch_count)
            ]
        block = blocks[0].reshape(batch_count, per_owner, -1)
        block = lax.all_to_all(block, "batch", split_axis=0, concat_axis=0, tiled=True)
        return [block.reshape(targets, -1)]

    order = [0] + list(range(n_msg - 1, 0, -1))
    arrived = exchange(msgs)
    arrived = [arrived[k] for k in order]

    in_hbm = pl.BlockSpec(memory_space=pltpu.HBM)
    one_state = session_head_state.shape[1:]
    middle = sessions
    small = pltpu.CompilerParams(vmem_limit_bytes=4 << 20)

    def cost(count):
        elements = count * heads * HEAD_CHANNELS * state_size
        return pl.CostEstimate(flops=8 * elements, bytes_accessed=4 * elements, transcendentals=0)

    made = pl.pallas_call(
        functools.partial(state_kernel, 0),
        out_shape=pltpu.VMEM((middle,) + one_state, BF16),
        in_specs=[vmem()] * 4,
        out_specs=vmem(),
        compiler_params=small,
        cost_estimate=cost(middle),
        name="state",
    )(left, b_rows, keep, held_state)
    arrived, made = lax.optimization_barrier((arrived, made))

    partial, pick = pl.pallas_call(
        functools.partial(down_kernel, order),
        out_shape=[shape((targets, 2 * RANK), F32), shape((targets, LANES), F32)],
        in_specs=[vmem()] * (n_msg + 2),
        out_specs=[vmem()] * 2,
        compiler_params=pltpu.CompilerParams(vmem_limit_bytes=4 << 20),
        name="down",
    )(*arrived, adapter_down_weight, squares)

    if tensor_count in (2, 4):
        parts = [partial] + [
            lax.ppermute(partial, "tensor", [(i, i ^ k) for i in range(tensor_count)])
            for k in range(1, tensor_count)
        ]
    else:
        parts = [lax.psum(partial, "tensor")]

    out = pl.pallas_call(
        functools.partial(up_kernel, len(parts), n_msg, sessions),
        out_shape=[shape((msg_rows, channels), BF16)] * n_msg + [shape((rows, LANES), F32)],
        in_specs=[vmem()] * (len(parts) + 2),
        out_specs=[vmem()] * (n_msg + 1),
        compiler_params=pltpu.CompilerParams(vmem_limit_bytes=4 << 20),
        name="up",
    )(*parts, pick, adapter_up_weight)
    terms, inverse = out[:n_msg], out[n_msg]
    returned = exchange(terms)
    returned = [returned[k] for k in order]

    normed, updated = pl.pallas_call(
        close_kernel,
        out_shape=[
            pltpu.HBM((DECODE_STEPS, sessions, channels), BF16),
            pltpu.HBM(session_head_state.shape, BF16),
        ],
        in_specs=[vmem()] * 4,
        out_specs=[in_hbm, in_hbm],
        scratch_shapes=[
            pltpu.VMEM((DECODE_STEPS, sessions, channels), BF16),
            pltpu.SemaphoreType.DMA((2,)),
        ],
        compiler_params=small,
        cost_estimate=cost(sessions),
        name="close",
    )(gated, inverse, gain, made)

    delta = pl.pallas_call(
        functools.partial(final_kernel, order),
        out_shape=shape((DECODE_STEPS, sessions, channels), F32),
        in_specs=[vmem()] * (n_msg + 2),
        out_specs=vmem(),
        compiler_params=pltpu.CompilerParams(vmem_limit_bytes=4 << 20),
        name="final",
    )(*returned, place, inverse)
    return (updated, normed, delta)


def solution(mesh):
    placed = (
        P(("groups", "batch"), "tensor", None, None),
        P(None, ("groups", "batch"), "tensor"),
        P(None, ("groups", "batch"), "tensor"),
        P(None, ("groups", "batch"), None, None),
        P(None, ("groups", "batch"), None, None),
        P(None, ("groups", "batch"), "tensor"),
        P("tensor"),
        P("tensor"),
        P("tensor"),
        P("tensor"),
        P(("groups", "batch"), None, "tensor"),
        P(("groups", "batch"), None, "tensor"),
        P(("groups", "batch")),
        P("groups"),
    )
    return jax.shard_map(
        per_device,
        mesh=mesh,
        in_specs=placed,
        out_specs=(
            P(("groups", "batch"), "tensor", None, None),
            P(None, ("groups", "batch"), "tensor"),
            P(None, ("groups", "batch"), "tensor"),
        ),
        check_vma=False,
    )
```
